512 devices in a mesh: gx: 16 (over z, y_lo), gy: 8 (over y_hi, core), gz: 4 (over x).
Axes of the slice: x: 4, y: 8 (y_hi: 4, y_lo: 2; y = y_hi * 2 + y_lo), z: 8, core: 2. Of those that a mesh axis runs over, the one named last changes fastest.
Arguments:
- features: bfloat16 [32, 64, 32, 512], P(None, 'gx', 'gy', 'gz'), may hold values from -6 to 6
- cotangent: bfloat16 [32, 64, 32, 512], P(None, 'gx', 'gy', 'gz'), may hold values from -6 to 6
- w_fine_in: bfloat16 [27, 32, 32], replicated, may hold values from -0.21875 to 0.21875
- w_coarse_in: bfloat16 [27, 32, 128], replicated, may hold values from -0.21875 to 0.21875
- w_coarse_mid: bfloat16 [27, 128, 128], replicated, may hold values from -0.109375 to 0.109375
- w_lift: bfloat16 [128, 32], replicated, may hold values from -0.5 to 0.5
- w_fine_out: bfloat16 [27, 32, 32], replicated, may hold values from -0.21875 to 0.21875
Outputs:
- output: bfloat16 [32, 64, 32, 512], P(None, 'gx', 'gy', 'gz')
- grad_input: bfloat16 [32, 64, 32, 512], P(None, 'gx', 'gy', 'gz')
- grad_fine_in: float32 [27, 32, 32], P(None, 'gx', ('gy', 'gz'))
- grad_coarse_in: float32 [27, 32, 128], P(None, 'gx', ('gy', 'gz'))
- grad_coarse_mid: float32 [27, 128, 128], P(None, 'gx', ('gy', 'gz'))
- grad_lift: float32 [128, 32], P('gx', ('gy', 'gz'))
- grad_fine_out: float32 [27, 32, 32], P(None, 'gx', ('gy', 'gz'))
The draws below stay inside these ranges and needn't reach their ends.
All inputs are finite; a program needn't handle non-finite values.
Results may differ from the reference program's by a relative error of at most 0.02.
Values may be sent and summed in bfloat16 or wider, within the bound.
No kernel may reach another device: no remote copies, remote signals or barrier semaphores. Data moves between devices by JAX's collectives and lax.ppermute only.
A program may use at most 128 MiB of HBM per device.

```python
import math
import jax
import jax.numpy as jnp
from jax import lax

C = 32
CC = 128
NX = 64
NY = 32
NZ = 512


def levels(rng, dims, shards, least, top_value):
    loudness = 1.0
    for axis_at, shards_of in shards:
        heights = jax.random.uniform(jax.random.fold_in(jax.random.fold_in(rng, 6), axis_at), (shards_of,), jnp.float32, least / len(shards), top_value / len(shards))
        loudness = loudness * jnp.repeat(jnp.exp(heights), dims[axis_at] // shards_of).reshape((-1,) + (1,) * (len(dims) - 1 - axis_at))
    return loudness


def scatter_about(rng, shape, scale, reach, pieces=(), kind=jnp.bfloat16):
    values = jax.random.normal(rng, shape, jnp.float32) * scale
    if len(pieces) > 0:
        values = levels(rng, shape, pieces, -0.22, 0.18) * values
    return jnp.clip(values, min=-reach, max=reach).astype(kind)


def setup_inputs(seed: int = 0) -> dict:
    key_of = jax.random.split(jax.random.key(seed), 8)
    return {
        "features": scatter_about(key_of[0], (C, NX, NY, NZ), 1.0, 6.0, ((1, 16), (2, 8), (3, 4))),
        "cotangent": scatter_about(key_of[1], (C, NX, NY, NZ), 1.0, 6.0, ((1, 16), (2, 8), (3, 4))),
        "w_fine_in": scatter_about(key_of[2], (27, C, C), (27 * C) ** -0.5, 0.21875),
        "w_coarse_in": scatter_about(key_of[3], (27, C, CC), (27 * C) ** -0.5, 0.21875),
        "w_coarse_mid": scatter_about(key_of[4], (27, CC, CC), (27 * CC) ** -0.5, 0.109375),
        "w_lift": scatter_about(key_of[5], (CC, C), CC ** -0.5, 0.5),
        "w_fine_out": scatter_about(key_of[6], (27, C, C), (27 * C) ** -0.5, 0.21875),
    }


def conv_full(field, weight):
    cin = weight.shape[1]
    cout = weight.shape[2]
    kernel = weight.astype(jnp.float32).reshape(3, 3, 3, cin, cout).transpose(4, 3, 0, 1, 2)
    result = lax.conv_general_dilated(field.astype(jnp.float32)[None], kernel, (1, 1, 1), [(1, 1), (1, 1), (1, 1)], dimension_numbers=('NCDHW', 'OIDHW', 'NCDHW'), precision=lax.Precision.HIGHEST)
    return result[0]

def conv_back(grad, weight):
    return conv_full(grad, jnp.flip(weight, 0).transpose(0, 2, 1))

def weight_grad(field, grad):
    cin = field.shape[0]
    cout = grad.shape[0]
    depth, height, length = (field.shape[1], field.shape[2], field.shape[3])
    padded = jnp.pad(field.astype(jnp.float32), ((0, 0), (1, 1), (1, 1), (1, 1)))
    flat_grad = grad.astype(jnp.float32).reshape(cout, -1)
    blocks = []
    for tap in range(27):
        shift_x, shift_y, shift_z = (tap // 9, tap // 3 % 3, tap % 3)
        window = padded[:, shift_x:shift_x + depth, shift_y:shift_y + height, shift_z:shift_z + length].reshape(cin, -1)
        blocks.append(lax.dot_general(window, flat_grad, (((1,), (1,)), ((), ())), precision=lax.Precision.HIGHEST))
    return jnp.stack(blocks)

def pool_blocks(field):
    chans, depth, height, length = field.shape
    grouped = field.astype(jnp.float32).reshape(chans, depth // 4, 4, height // 4, 4, length // 4, 4)
    return grouped.sum(axis=(2, 4, 6))

def spread_up(field):
    chans, depth, height, length = field.shape
    grown = jnp.broadcast_to(field[:, :, None, :, None, :, None], (chans, depth, 4, height, 4, length, 4))
    return grown.reshape(chans, depth * 4, height * 4, length * 4)

def silu_slope(values):
    sigma = jax.nn.sigmoid(values)
    return sigma * (1.0 + values * (1.0 - sigma))

def reference(features, cotangent, w_fine_in, w_coarse_in, w_coarse_mid, w_lift, w_fine_out):
    scale = 1.0 / math.sqrt(NX * NY * NZ)
    z_first = conv_full(features, w_fine_in)
    act_first = jax.nn.silu(z_first).astype(jnp.bfloat16)
    pooled = (pool_blocks(act_first) / 64.0).astype(jnp.bfloat16)
    z_second = conv_full(pooled, w_coarse_in)
    act_second = jax.nn.silu(z_second).astype(jnp.bfloat16)
    z_third = conv_full(act_second, w_coarse_mid)
    act_third = jax.nn.silu(z_third).astype(jnp.bfloat16)
    lift_f = w_lift.astype(jnp.float32)
    third_f = act_third.astype(jnp.float32)
    lifted = jnp.tensordot(lift_f, third_f, axes=((0,), (0,)), precision=lax.Precision.HIGHEST)
    joined = (act_first.astype(jnp.float32) + spread_up(lifted)).astype(jnp.bfloat16)
    output = conv_full(joined, w_fine_out).astype(jnp.bfloat16)
    grad_fine_out = weight_grad(joined, cotangent) * scale
    d_joined = conv_back(cotangent, w_fine_out)
    d_lift = pool_blocks(d_joined)
    grad_lift = jnp.tensordot(third_f, d_lift, axes=((1, 2, 3), (1, 2, 3)), precision=lax.Precision.HIGHEST) * scale
    d_third = jnp.tensordot(lift_f, d_lift, axes=((1,), (0,)), precision=lax.Precision.HIGHEST)
    dz_third = (d_third * silu_slope(z_third)).astype(jnp.bfloat16)
    grad_coarse_mid = weight_grad(act_second, dz_third) * scale
    dz_second = (conv_back(dz_third, w_coarse_mid) * silu_slope(z_second)).astype(jnp.bfloat16)
    grad_coarse_in = weight_grad(pooled, dz_second) * scale
    d_pool = conv_back(dz_second, w_coarse_in)
    dz_first = ((d_joined + spread_up(d_pool) / 64.0) * silu_slope(z_first)).astype(jnp.bfloat16)
    grad_fine_in = weight_grad(features, dz_first) * scale
    grad_input = conv_back(dz_first, w_fine_in).astype(jnp.bfloat16)
    return (output, grad_input, grad_fine_in, grad_coarse_in, grad_coarse_mid, grad_lift, grad_fine_out)
```

```python
import functools
import math

import jax
import jax.numpy as jnp
import numpy as np
from jax import lax
from jax.experimental import pallas as pl
from jax.experimental.pallas import tpu as pltpu
from jax.sharding import Mesh
from jax.sharding import PartitionSpec as P

GX = ("gx_0", "gx_1")
INTERPRET = False
VMEM_BYTES = 44 * 1024 * 1024
BF = jnp.bfloat16
F32 = jnp.float32
PAD = 5
OWN = 32
PITCH = 48
NT = (((1,), (1,)), ((), ()))
TN = (((0,), (0,)), ((), ()))
COARSE_OF = (0, 1, 1, 1, 1, 2)


def mm(lhs, rhs):
    return jnp.dot(lhs, rhs, preferred_element_type=F32)


def mm_nt(lhs, rhs):
    return lax.dot_general(lhs, rhs, NT, preferred_element_type=F32)


def mm_tn(lhs, rhs):
    return lax.dot_general(lhs, rhs, TN, preferred_element_type=F32)


def lane_roll(value, shift):
    return pltpu.roll(value, shift % value.shape[1], 1)


def row_roll(value, shift):
    return pltpu.roll(value, shift % value.shape[0], 0)


def call(body, out_shape, scratch, n_in, smem_first):
    spec = [pl.BlockSpec(memory_space=pltpu.VMEM)] * n_in
    if smem_first:
        spec[0] = pl.BlockSpec(memory_space=pltpu.SMEM)
    return pl.pallas_call(
        body,
        out_shape=out_shape,
        in_specs=spec,
        out_specs=jax.tree.map(lambda _: pl.BlockSpec(memory_space=pltpu.VMEM), out_shape),
        scratch_shapes=scratch,
        compiler_params=pltpu.CompilerParams(vmem_limit_bytes=VMEM_BYTES),
        interpret=INTERPRET,
    )


def rows_of(own, xlo, xhi, ylo, yhi):
    def row(arr, xi, yi):
        if yi < 2:
            return ylo[arr, xi, yi]
        if yi >= 6:
            return yhi[arr, xi, yi - 6]
        if xi < 2:
            return xlo[arr, xi, yi - 2]
        if xi >= 6:
            return xhi[arr, xi - 6, yi - 2]
        return own[arr, xi - 2, yi - 2]

    return row


def z_faces(own, xlo, xhi, ylo, yhi, perm, out):
    row = rows_of(own, xlo, xhi, ylo, yhi)
    lane = lax.broadcasted_iota(jnp.int32, (32, 128), 1)
    for arr in range(2):
        halves = []
        for half in range(2):
            gathered = jnp.zeros((32, 128), F32)
            for at in range(32):
                cell = half * 32 + at
                value = row(arr, cell // 8, cell % 8).astype(F32)
                moved = lane_roll(value, 4 * at + 2)
                here = (lane >= 4 * at) & (lane < 4 * at + 4)
                gathered = jnp.where(here, moved, gathered)
            halves.append(gathered.astype(BF))
        tiles = mm(jnp.concatenate(halves, axis=1), perm[...]).astype(BF)
        out[arr, 0] = tiles[:, :128]
        out[arr, 1] = tiles[:, 128:]


def face_perm():
    perm = np.zeros((256, 256), np.float32)
    for cell in range(64):
        perm[4 * cell + 0, cell] = 1
        perm[4 * cell + 3, 64 + cell] = 1
        perm[4 * cell + 1, 128 + cell] = 1
        perm[4 * cell + 2, 192 + cell] = 1
    return jnp.asarray(perm, BF)


def stacked_row(value, edge, cell, lane):
    before = jnp.where(lane == 0, lane_roll(edge, -cell), lane_roll(value, 1))
    after = jnp.where(lane == 127, lane_roll(edge, 63 - cell), lane_roll(value, -1))
    return jnp.concatenate([before, value, after], axis=0).astype(BF)


def edge_sum(weight, tile):
    product = mm(weight, tile)
    total = None
    for ab in range(9):
        part = lane_roll(product[ab * 32 : ab * 32 + 32], -(ab // 3 * 8 + ab % 3))
        total = part if total is None else total + part
    return total


def slope_of(value):
    sigma = jax.nn.sigmoid(value)
    return sigma, sigma * (1.0 + value * (1.0 - sigma))


def fine_first(
    sizes, place, own, xlo, xhi, ylo, yhi, face, face_l, face_r, w_z, w_d, pool,
    act, slope, d_join, act_e, slope_e, d_join_e, msg, acc, vbuf,
):
    count_x, count_y, count_z = sizes
    gx, gy, gz = place[0], place[1], place[2]
    row = rows_of(own, xlo, xhi, ylo, yhi)
    lane = lax.broadcasted_iota(jnp.int32, (32, 128), 1)
    lower = lane < 64
    x_in = [gx > 0, None, None, None, None, gx < count_x - 1]
    y_in = [gy > 0, None, None, None, None, gy < count_y - 1]

    def factor(flag):
        return 1.0 if flag is None else jnp.where(flag, 1.0, 0.0)

    pooled = {}
    for arr, weight in ((0, w_z), (1, w_d)):
        tile_a, tile_b = face[arr, 0].astype(F32), face[arr, 1].astype(F32)
        left_a, left_b = face_l[arr, 0].astype(F32), face_l[arr, 1].astype(F32)
        right_a, right_b = face_r[arr, 0].astype(F32), face_r[arr, 1].astype(F32)
        swapped = lane_roll(tile_b, 64)
        edge_0 = jnp.where(lower, left_a, swapped)
        edge_1 = jnp.where(lower, left_b, right_b)
        edge_2 = jnp.where(lower, swapped, right_a)
        edges = edge_sum(weight[...], jnp.concatenate([edge_0, edge_1, edge_2], axis=0).astype(BF))
        for m in range(6):
            acc[m] = jnp.zeros((32, 768), F32)
        for xi in range(8):
            for yi in range(8):
                value = row(arr, xi, yi).astype(F32)
                vbuf[:, yi * 128 : yi * 128 + 128] = stacked_row(value, edge_1, xi * 8 + yi, lane)
            product = mm(weight[...], vbuf[...])
            for a in range(3):
                m = xi - a
                if 0 <= m < 6:
                    part = None
                    for b in range(3):
                        at = (3 * a + b) * 32
                        piece = product[at : at + 32, b * 128 : b * 128 + 768]
                        part = piece if part is None else part + piece
                    acc[m] = acc[m] + part
        total = jnp.zeros((32, 128), F32)
        if arr == 0:
            x_at = lax.broadcasted_iota(jnp.int32, (32, 128), 1) % 64 // 8
            y_at = lax.broadcasted_iota(jnp.int32, (32, 128), 1) % 8
            inside = jnp.where(lower, factor(gz > 0), factor(gz < count_z - 1))
            inside = inside * jnp.where(x_at == 0, factor(x_in[0]), 1.0)
            inside = inside * jnp.where(x_at == 5, factor(x_in[5]), 1.0)
            inside = inside * jnp.where(y_at == 0, factor(y_in[0]), 1.0)
            inside = inside * jnp.where(y_at == 5, factor(y_in[5]), 1.0)
            sigma, steep = slope_of(edges)
            act_e[...] = (edges * sigma * inside).astype(BF).astype(F32)
            slope_e[...] = steep * inside
            for m in range(6):
                for k in range(6):
                    at = slice(k * 128, k * 128 + 128)
                    mask = factor(x_in[m]) * factor(y_in[k])
                    value = acc[m, :, at]
                    sigma, steep = slope_of(value)
                    first = (value * sigma * mask).astype(BF)
                    act[m, :, at] = first
                    slope[m, :, at] = steep * mask
                    if 1 <= m < 5 and 1 <= k < 5:
                        total = total + first.astype(F32)
            total = total * (1.0 / 64.0)
        else:
            d_join_e[...] = edges
            for m in range(6):
                d_join[m] = acc[m]
                if 1 <= m < 5:
                    for k in range(1, 5):
                        total = total + acc[m, :, k * 128 : k * 128 + 128]
        pooled[arr] = lax.dot_general(
            pool[...], total, NT, preferred_element_type=F32, precision=lax.Precision.HIGHEST
        )
    msg[...] = jnp.concatenate([pooled[0], pooled[1]], axis=1).astype(BF)


def coarse(
    sizes, scale, place, recv, w_in, w_mid, w_lift, w_lift_64,
    g_mid, g_in, g_lift, out_ld,
    raw, p3, c3, d3, e3, s2, c2, ws_mid, ws_in, lds,
):
    count_x, count_y, count_z = sizes
    gx, gy, gz = place[0], place[1], place[2]
    rows = count_y * PITCH
    body_rows = slice(PITCH, PITCH + rows)

    z_at = lax.broadcasted_iota(jnp.int32, (PITCH, 128), 0)
    z_all = z_at + (gz * OWN - PAD)
    z_mask = jnp.where((z_all >= 0) & (z_all < count_z * OWN), 1.0, 0.0)
    z_mask = jnp.concatenate([z_mask] * count_y, axis=0)
    own_mask = jnp.where((z_at >= PAD) & (z_at < PAD + OWN), 1.0, 0.0)
    own_mask = jnp.concatenate([own_mask] * count_y, axis=0)

    for store in (p3, c3, d3, e3):
        for plane in range(store.shape[0]):
            blank = jnp.zeros((PITCH, store.shape[2]), BF)
            store[plane, 0:PITCH] = blank
            store[plane, PITCH + rows : 2 * PITCH + rows] = blank
    lds[...] = jnp.zeros(lds.shape, F32)
    for tap in range(27):
        at = tap % 3 * 128
        ws_mid[tap // 3, :, at : at + 128] = w_mid[26 - tap]
        ws_in[tap // 3, :, at : at + 128] = w_in[26 - tap]

    def inside(plane):
        at = gx + plane - PAD
        return (at >= 0) & (at < count_x), jnp.clip(at, 0, count_x - 1)

    def stacked(value):
        return jnp.concatenate([row_roll(value, 1), value, row_roll(value, -1)], axis=1).astype(BF)

    def unpack(plane, carry):
        ok, at = inside(plane)
        keep = jnp.where(ok, 1.0, 0.0)
        parts = []
        for y in range(count_y):
            block = recv[at, y].astype(F32) * keep
            parts.append(block[:, :64])
            parts.append(block[:, 64:])
        whole = jnp.concatenate(parts, axis=0)
        raw[plane] = whole.astype(BF)
        p3[plane, body_rows, :] = stacked(whole[:, :32])
        return carry

    lax.fori_loop(0, 11, unpack, 0)

    def taps(store, first, weight, product):
        total = None
        for ab in range(9):
            a, b = ab // 3, ab % 3
            part = product(store[first + a, b * PITCH : b * PITCH + rows, :], weight(ab))
            total = part if total is None else total + part
        return total

    def level_2(plane, carry):
        ok, _ = inside(plane)
        mask = z_mask * jnp.where(ok, 1.0, 0.0)
        z_2 = taps(p3, plane - 1, lambda ab: w_in_ref(ab), mm)
        sigma, steep = slope_of(z_2)
        s2[plane - 1] = steep * mask
        c3[plane - 1, body_rows, :] = stacked(z_2 * sigma * mask)
        return carry

    def w_in_ref(ab):
        return jnp.concatenate([w_in[3 * ab], w_in[3 * ab + 1], w_in[3 * ab + 2]], axis=0)

    def w_mid_ref(ab):
        return jnp.concatenate([w_mid[3 * ab], w_mid[3 * ab + 1], w_mid[3 * ab + 2]], axis=0)

    lax.fori_loop(1, 10, level_2, 0)

    def level_3(plane, carry):
        ok, _ = inside(plane)
        mask = z_mask * jnp.where(ok, 1.0, 0.0)
        z_3 = taps(c3, plane - 2, lambda ab: w_mid_ref(ab), mm)
        sigma, steep = slope_of(z_3)
        c2[plane - 2] = (z_3 * sigma * mask).astype(BF)
        d_third = mm_nt(raw[plane], w_lift_64[...])
        d3[plane - 2, body_rows, :] = stacked(d_third * steep)
        return carry

    lax.fori_loop(2, 9, level_3, 0)

    def level_2_back(plane, carry):
        total = taps(d3, plane - 3, lambda ab: ws_mid[ab], mm_nt)
        e3[plane - 3, body_rows, :] = stacked(total * s2[plane - 1])
        return carry

    lax.fori_loop(3, 8, level_2_back, 0)

    def level_1_back(plane, carry):
        d_pool = taps(e3, plane - 4, lambda ab: ws_in[ab], mm_nt)
        lifted = mm(c2[plane - 2], w_lift[...])
        both = jnp.concatenate([lifted, d_pool], axis=1)
        for y in range(count_y):
            lds[plane - 4, 1 + y] = both[y * PITCH : y * PITCH + PITCH]
        return carry

    lax.fori_loop(4, 7, level_1_back, 0)
    for i in range(3):
        for j in range(3):
            out_ld[i, j] = lds[i, gy + j]

    span = 128 // count_y
    pick = lax.broadcasted_iota(jnp.int32, (span, 128), 1)
    pick = pick == lax.broadcasted_iota(jnp.int32, (span, 128), 0) + gy * span
    pick = jnp.where(pick, 1.0, 0.0).astype(BF)
    dz3 = (d3[3, body_rows, 128:256].astype(F32) * own_mask).astype(BF)
    dz3 = mm_nt(pick, dz3).astype(BF)
    dz2 = (e3[2, body_rows, 128:256].astype(F32) * own_mask).astype(BF)
    dz2 = mm_nt(pick, dz2).astype(BF)
    for ab in range(9):
        a, b = ab // 3, ab % 3
        at = slice(b * PITCH, b * PITCH + rows)
        g_mid[ab] = mm(dz3, c3[3 + a, at, :]) * scale
        g_in[ab] = mm(dz2, p3[4 + a, at, :]) * scale
    lift_rows = g_lift.shape[0]
    pick = lax.broadcasted_iota(jnp.int32, (lift_rows, 64), 1)
    pick = pick == lax.broadcasted_iota(jnp.int32, (lift_rows, 64), 0) + (32 + gy * (32 // count_y))
    pick = jnp.where(pick, 1.0, 0.0).astype(BF)
    d_lift = mm_nt(pick, raw[5]).astype(BF)
    third = (c2[3].astype(F32) * own_mask).astype(BF)
    g_lift[...] = mm(d_lift, third) * scale


def up_matrix():
    up = np.zeros((PITCH, 128), np.float32)
    for lane in range(128):
        up[PAD + lane // 4, lane] = 1
    return jnp.asarray(np.concatenate([up, up], axis=0), BF)


def edge_matrix():
    edge = np.zeros((24, 128), np.float32)
    for side in range(2):
        for x in range(6):
            for y in range(6):
                source = side * 9 + COARSE_OF[x] * 3 + COARSE_OF[y]
                edge[source, side * 64 + x * 8 + y] = 1
    return jnp.asarray(np.concatenate([edge, edge], axis=0), BF)


def split_two(value):
    high = value.astype(BF)
    low = (value - high.astype(F32)).astype(BF)
    return jnp.concatenate([high, low], axis=0)


def fine_second(
    scale, own, act, slope, d_join, act_e, slope_e, d_join_e, ld, up, edge_up, w_o, w_g,
    out, g_in, g_out_w, g_in_w, v_join, v_dz, acc, edge_rows,
):
    lane = lax.broadcasted_iota(jnp.int32, (32, 128), 1)
    spread = {}
    for x in range(3):
        for y in range(3):
            spread[x, y] = mm_tn(split_two(ld[x, y]), up[...])
    edge_rows[...] = jnp.zeros(edge_rows.shape, F32)
    for side in range(2):
        for x in range(3):
            for y in range(3):
                at = side * 9 + x * 3 + y
                z = PAD - 1 if side == 0 else PAD + OWN
                edge_rows[at : at + 1, :] = ld[x, y, z : z + 1, :]
    spread_e = mm_tn(split_two(edge_rows[...]), edge_up[...])
    join_e = (act_e[...] + spread_e[:32]).astype(BF).astype(F32)
    dz_e = ((d_join_e[...] + spread_e[32:] * (1.0 / 64.0)) * slope_e[...]).astype(BF).astype(F32)
    for m in range(6):
        for k in range(6):
            at = slice(k * 128, k * 128 + 128)
            over = spread[COARSE_OF[m], COARSE_OF[k]]
            join = (act[m, :, at].astype(F32) + over[:32]).astype(BF).astype(F32)
            v_join[m, :, at] = stacked_row(join, join_e, m * 8 + k, lane)
            dz = (d_join[m, :, at] + over[32:] * (1.0 / 64.0)) * slope[m, :, at]
            v_dz[m, :, at] = stacked_row(dz.astype(BF).astype(F32), dz_e, m * 8 + k, lane)
    for store, weight, result in ((v_join, w_o, out), (v_dz, w_g, g_in)):
        for x in range(4):
            acc[x] = jnp.zeros((32, 512), F32)
        for m in range(6):
            product = mm(weight[...], store[m])
            for a in range(3):
                x = m - a
                if 0 <= x < 4:
                    part = None
                    for b in range(3):
                        at = (3 * a + b) * 32
                        piece = product[at : at + 32, b * 128 : b * 128 + 512]
                        part = piece if part is None else part + piece
                    acc[x] = acc[x] + part
        for x in range(4):
            for y in range(4):
                result[x, y] = acc[x, :, y * 128 : y * 128 + 128].astype(BF)
    flat = [
        [jnp.concatenate([own[arr, x, y] for y in range(4)], axis=1) for x in range(4)]
        for arr in range(2)
    ]
    for ab in range(9):
        a, b = ab // 3, ab % 3
        at = slice(b * 128, b * 128 + 512)
        total_o = None
        total_i = None
        for x in range(4):
            part_o = mm_nt(flat[1][x], v_join[x + a, :, at])
            part_i = mm_nt(v_dz[x + a, :, at], flat[0][x])
            total_o = part_o if total_o is None else total_o + part_o
            total_i = part_i if total_i is None else total_i + part_i
        g_out_w[ab] = total_o * scale
        by_tap = [total_i[c * 32 : c * 32 + 32] for c in range(3)]
        g_in_w[ab] = jnp.concatenate(by_tap, axis=1) * scale


def from_below(value, axis):
    count = lax.axis_size(axis)
    return lax.ppermute(value, axis, [(i, i + 1) for i in range(count - 1)])


def from_above(value, axis):
    count = lax.axis_size(axis)
    return lax.ppermute(value, axis, [(i + 1, i) for i in range(count - 1)])


def forward_taps(weight):
    return weight.reshape(9, 3, 32, 32).transpose(0, 3, 1, 2).reshape(288, 96)


def backward_taps(weight):
    return jnp.flip(weight, 0).reshape(9, 3, 32, 32).transpose(0, 2, 1, 3).reshape(288, 96)


def shape_of(shape, dtype):
    return jax.ShapeDtypeStruct(shape, dtype)


def shards(features, cotangent, w_fine_in, w_coarse_in, w_coarse_mid, w_lift, w_fine_out):
    sizes = (lax.axis_size(GX), lax.axis_size("gy"), lax.axis_size("gz"))
    count_x, count_y, count_z = sizes
    cells = count_x * count_y * count_z * 4 * 4 * 128
    scale = 1.0 / math.sqrt(cells)
    place = jnp.stack([lax.axis_index(GX), lax.axis_index("gy"), lax.axis_index("gz")])
    place = place.astype(jnp.int32)

    own = jnp.stack([features, cotangent]).transpose(0, 2, 3, 1, 4)
    xlo = from_below(own[:, 2:4], GX)
    xhi = from_above(own[:, 0:2], GX)
    y_tail = jnp.concatenate([xlo[:, :, 2:4], own[:, :, 2:4], xhi[:, :, 2:4]], axis=1)
    y_head = jnp.concatenate([xlo[:, :, 0:2], own[:, :, 0:2], xhi[:, :, 0:2]], axis=1)
    ylo = from_below(y_tail, "gy")
    yhi = from_above(y_head, "gy")
    face = call(z_faces, shape_of((2, 2, 32, 128), BF), [], 6, False)(
        own, xlo, xhi, ylo, yhi, face_perm()
    )
    face_l = from_below(face, "gz")
    face_r = from_above(face, "gz")

    pool = np.zeros((32, 128), np.float32)
    for at in range(128):
        pool[at // 4, at] = 1
    act, slope, d_join, act_e, slope_e, d_join_e, msg = call(
        functools.partial(fine_first, sizes),
        (
            shape_of((6, 32, 768), BF),
            shape_of((6, 32, 768), F32),
            shape_of((6, 32, 768), F32),
            shape_of((32, 128), F32),
            shape_of((32, 128), F32),
            shape_of((32, 128), F32),
            shape_of((32, 64), BF),
        ),
        [pltpu.VMEM((6, 32, 768), F32), pltpu.VMEM((96, 1024), BF)],
        12,
        True,
    )(
        place, own, xlo, xhi, ylo, yhi, face, face_l, face_r,
        forward_taps(w_fine_in), backward_taps(w_fine_out), jnp.asarray(pool),
    )

    z_lo = from_below(msg[24:32], "gz")
    z_hi = from_above(msg[0:8], "gz")
    window = jnp.concatenate(
        [z_lo[8 - PAD :], msg, z_hi[:PAD], jnp.zeros((PITCH - OWN - 2 * PAD, 64), BF)], axis=0
    )
    packed = jnp.concatenate([window[:24], window[24:]], axis=1)
    plane_axes = GX + ("gy",)
    recv = lax.all_to_all(
        jnp.broadcast_to(packed[None], (count_x * count_y, 24, 128)),
        plane_axes,
        split_axis=0,
        concat_axis=0,
        tiled=True,
    ).reshape(count_x, count_y, 24, 128)

    rows = count_y * PITCH
    span = 128 // count_y
    lift_span = 32 // count_y
    g_mid, g_in, g_lift, ld = call(
        functools.partial(coarse, sizes, scale),
        (
            shape_of((9, span, 384), F32),
            shape_of((9, span, 96), F32),
            shape_of((max(8, lift_span), 128), F32),
            shape_of((3, 3, PITCH, 64), F32),
        ),
        [
            pltpu.VMEM((11, rows, 64), BF),
            pltpu.VMEM((11, rows + 2 * PITCH, 96), BF),
            pltpu.VMEM((9, rows + 2 * PITCH, 384), BF),
            pltpu.VMEM((7, rows + 2 * PITCH, 384), BF),
            pltpu.VMEM((5, rows + 2 * PITCH, 384), BF),
            pltpu.VMEM((9, rows, 128), F32),
            pltpu.VMEM((7, rows, 128), BF),
            pltpu.VMEM((9, 128, 384), BF),
            pltpu.VMEM((9, 32, 384), BF),
            pltpu.VMEM((3, count_y + 2, PITCH, 64), F32),
        ],
        6,
        True,
    )(
        place, recv, w_coarse_in, w_coarse_mid, w_lift,
        jnp.concatenate([jnp.zeros((128, 32), BF), w_lift], axis=1),
    )

    out, grad_input, g_fo, g_fi = call(
        functools.partial(fine_second, scale),
        (
            shape_of((4, 4, 32, 128), BF),
            shape_of((4, 4, 32, 128), BF),
            shape_of((9, 32, 96), F32),
            shape_of((9, 32, 96), F32),
        ),
        [
            pltpu.VMEM((6, 96, 768), BF),
            pltpu.VMEM((6, 96, 768), BF),
            pltpu.VMEM((4, 32, 512), F32),
            pltpu.VMEM((24, 64), F32),
        ],
        12,
        False,
    )(
        own, act, slope, d_join, act_e, slope_e, d_join_e, ld, up_matrix(), edge_matrix(),
        forward_taps(w_fine_out), backward_taps(w_fine_in),
    )
    out = out.transpose(2, 0, 1, 3)
    grad_input = grad_input.transpose(2, 0, 1, 3)

    fine = jnp.stack([g_fo, g_fi]).reshape(2, 9, count_y, 32 // count_y, 96)
    fine = fine.transpose(2, 0, 1, 3, 4)
    fine = lax.all_to_all(fine, "gy", split_axis=0, concat_axis=0, tiled=True).sum(axis=0)

    def blocks(value, o_each, i_each):
        value = value.reshape(9, count_z, o_each, 3, count_x, i_each)
        value = value.transpose(4, 1, 0, 3, 5, 2)
        return value.reshape(count_x, count_z, -1)

    i_fine = 32 // count_x
    o_fine = 32 // (count_y * count_z)
    i_mid = 128 // count_x
    o_mid = 128 // (count_y * count_z)
    lift = g_lift[:lift_span].reshape(count_z, o_fine, count_x, i_mid).transpose(2, 0, 3, 1)
    pieces = [
        blocks(g_mid, o_mid, i_mid),
        blocks(g_in, o_mid, i_fine),
        blocks(fine[0], o_fine, i_fine),
        blocks(fine[1], o_fine, i_fine),
        lift.reshape(count_x, count_z, -1),
    ]
    widths = [piece.shape[2] for piece in pieces]
    joint = jnp.concatenate(pieces, axis=2).reshape(count_x * count_z, -1)
    joint = lax.all_to_all(joint, GX + ("gz",), split_axis=0, concat_axis=0, tiled=True)
    joint = joint.sum(axis=0)
    ends = np.cumsum([0] + widths)
    flat = [joint[ends[at] : ends[at + 1]] for at in range(5)]
    grad_coarse_mid = flat[0].reshape(27, i_mid, o_mid)
    grad_coarse_in = flat[1].reshape(27, i_fine, o_mid)
    grad_fine_out = flat[2].reshape(27, i_fine, o_fine)
    grad_fine_in = jnp.flip(flat[3].reshape(27, i_fine, o_fine), 0)
    grad_lift = flat[4].reshape(i_mid, o_fine)
    return (
        out,
        grad_input,
        grad_fine_in,
        grad_coarse_in,
        grad_coarse_mid,
        grad_lift,
        grad_fine_out,
    )


def solution(mesh):
    split = Mesh(
        mesh.devices.reshape(mesh.shape["gx"] // 2, 2, mesh.shape["gy"], mesh.shape["gz"]),
        ("gx_0", "gx_1", "gy", "gz"),
    )
    return jax.shard_map(
        shards,
        mesh=split,
        in_specs=(P(None, GX, "gy", "gz"), P(None, GX, "gy", "gz"), P(), P(), P(), P(), P()),
        out_specs=(
            P(None, GX, "gy", "gz"),
            P(None, GX, "gy", "gz"),
            P(None, GX, ("gy", "gz")),
            P(None, GX, ("gy", "gz")),
            P(None, GX, ("gy", "gz")),
            P(GX, ("gy", "gz")),
            P(None, GX, ("gy", "gz")),
        ),
        check_vma=False,
    )
```

```python
import functools
import math

import jax
import jax.numpy as jnp
import numpy as np
from jax import lax
from jax.experimental import pallas as pl
from jax.experimental.pallas import tpu as pltpu
from jax.sharding import Mesh
from jax.sharding import PartitionSpec as P

GX = ("gx_0", "gx_1")
INTERPRET = False
BF = jnp.bfloat16
F32 = jnp.float32
PAD = 5
OWN = 32
PITCH = 48
NT = (((1,), (1,)), ((), ()))
TN = (((0,), (0,)), ((), ()))
COARSE_OF = (0, 1, 1, 1, 1, 2)


def mm(lhs, rhs):
    return jnp.dot(lhs, rhs, preferred_element_type=F32)


def mm_nt(lhs, rhs):
    return lax.dot_general(lhs, rhs, NT, preferred_element_type=F32)


def mm_tn(lhs, rhs):
    return lax.dot_general(lhs, rhs, TN, preferred_element_type=F32)


def lane_roll(value, shift):
    return pltpu.roll(value, shift % value.shape[1], 1)


def row_roll(value, shift):
    return pltpu.roll(value, shift % value.shape[0], 0)


def call(body, out_shape, scratch, n_in, smem_first, megabytes, keep_out=True):
    spec = [pl.BlockSpec(memory_space=pltpu.VMEM)] * n_in
    if smem_first:
        spec[0] = pl.BlockSpec(memory_space=pltpu.SMEM)
    out_spec = pl.BlockSpec(memory_space=pltpu.VMEM) if keep_out else pl.BlockSpec()
    return pl.pallas_call(
        body,
        out_shape=out_shape,
        in_specs=spec,
        out_specs=jax.tree.map(lambda _: out_spec, out_shape),
        scratch_shapes=scratch,
        compiler_params=pltpu.CompilerParams(vmem_limit_bytes=megabytes * 1024 * 1024),
        interpret=INTERPRET,
    )


def rows_of(own, xlo, xhi, ylo, yhi):
    def row(arr, xi, yi):
        if yi < 2:
            return ylo[arr, xi, yi]
        if yi >= 6:
            return yhi[arr, xi, yi - 6]
        if xi < 2:
            return xlo[arr, xi, yi - 2]
        if xi >= 6:
            return xhi[arr, xi - 6, yi - 2]
        return own[arr, xi - 2, yi - 2]

    return row


def iota(shape, dim):
    return lax.broadcasted_iota(jnp.int32, shape, dim)


def ones_where(flag):
    return jnp.where(flag, 1.0, 0.0)


def z_faces(own, xlo, xhi, ylo, yhi, out):
    row = rows_of(own, xlo, xhi, ylo, yhi)
    lane = iota((32, 128), 1)
    column = iota((256, 256), 1)
    source = jnp.where(column < 128, 0, 1)
    source = jnp.where(column % 128 < 64, source, 3 - source)
    perm = ones_where(iota((256, 256), 0) == column % 64 * 4 + source).astype(BF)
    for arr in range(2):
        halves = []
        for half in range(2):
            gathered = jnp.zeros((32, 128), F32)
            for at in range(32):
                cell = half * 32 + at
                value = row(arr, cell // 8, cell % 8).astype(F32)
                moved = lane_roll(value, 4 * at + 2)
                here = (lane >= 4 * at) & (lane < 4 * at + 4)
                gathered = jnp.where(here, moved, gathered)
            halves.append(gathered.astype(BF))
        tiles = mm(jnp.concatenate(halves, axis=1), perm).astype(BF)
        out[arr, 0] = tiles[:, :128]
        out[arr, 1] = tiles[:, 128:]


def stacked_row(value, edge, cell, lane):
    before = jnp.where(lane == 0, lane_roll(edge, -cell), lane_roll(value, 1))
    after = jnp.where(lane == 127, lane_roll(edge, 63 - cell), lane_roll(value, -1))
    return jnp.concatenate([before, value, after], axis=0).astype(BF)


def edge_sum(weight, tile):
    product = mm(weight, tile)
    total = None
    for ab in range(9):
        part = lane_roll(product[ab * 32 : ab * 32 + 32], -(ab // 3 * 8 + ab % 3))
        total = part if total is None else total + part
    return total


def slope_of(value):
    sigma = jax.nn.sigmoid(value)
    return sigma, sigma * (1.0 + value * (1.0 - sigma))


def forward_taps(weight, store):
    same = ones_where(iota((32, 32), 0) == iota((32, 32), 1)).astype(BF)
    for ab in range(9):
        stack = jnp.concatenate([weight[3 * ab + c] for c in range(3)], axis=0)
        store[ab * 32 : ab * 32 + 32, :] = mm_nt(same, stack).astype(BF)


def backward_taps(weight, store):
    for ab in range(9):
        stack = [weight[26 - 3 * ab - c].astype(F32) for c in range(3)]
        store[ab * 32 : ab * 32 + 32, :] = jnp.concatenate(stack, axis=1).astype(BF)


def fine_first(
    sizes, place, own, xlo, xhi, ylo, yhi, face, face_l, face_r, w_fine_in, w_fine_out,
    act, slope, d_join, edge, msg, acc, vbuf, w_z, w_d,
):
    count_x, count_y, count_z = sizes
    gx, gy, gz = place[0], place[1], place[2]
    row = rows_of(own, xlo, xhi, ylo, yhi)
    lane = iota((32, 128), 1)
    lower = lane < 64
    x_in = [gx > 0, None, None, None, None, gx < count_x - 1]
    y_in = [gy > 0, None, None, None, None, gy < count_y - 1]
    forward_taps(w_fine_in, w_z)
    backward_taps(w_fine_out, w_d)

    def factor(flag):
        return 1.0 if flag is None else jnp.where(flag, 1.0, 0.0)

    pooled = {}
    pool = ones_where(iota((32, 128), 1) // 4 == iota((32, 128), 0))
    for arr, weight in ((0, w_z), (1, w_d)):
        tile_a, tile_b = face[arr, 0].astype(F32), face[arr, 1].astype(F32)
        left_a, left_b = face_l[arr, 0].astype(F32), face_l[arr, 1].astype(F32)
        right_a, right_b = face_r[arr, 0].astype(F32), face_r[arr, 1].astype(F32)
        swapped = lane_roll(tile_b, 64)
        edge_0 = jnp.where(lower, left_a, swapped)
        edge_1 = jnp.where(lower, left_b, right_b)
        edge_2 = jnp.where(lower, swapped, right_a)
        edges = edge_sum(weight[...], jnp.concatenate([edge_0, edge_1, edge_2], axis=0).astype(BF))
        for m in range(6):
            acc[m] = jnp.zeros((32, 768), F32)
        for xi in range(8):
            for yi in range(8):
                value = row(arr, xi, yi).astype(F32)
                vbuf[:, yi * 128 : yi * 128 + 128] = stacked_row(value, edge_1, xi * 8 + yi, lane)
            product = mm(weight[...], vbuf[...])
            for a in range(3):
                m = xi - a
                if 0 <= m < 6:
                    part = None
                    for b in range(3):
                        at = (3 * a + b) * 32
                        piece = product[at : at + 32, b * 128 : b * 128 + 768]
                        part = piece if part is None else part + piece
                    acc[m] = acc[m] + part
        total = jnp.zeros((32, 128), F32)
        if arr == 0:
            x_at = lane % 64 // 8
            y_at = lane % 8
            inside = jnp.where(lower, factor(gz > 0), factor(gz < count_z - 1))
            inside = inside * jnp.where(x_at == 0, factor(x_in[0]), 1.0)
            inside = inside * jnp.where(x_at == 5, factor(x_in[5]), 1.0)
            inside = inside * jnp.where(y_at == 0, factor(y_in[0]), 1.0)
            inside = inside * jnp.where(y_at == 5, factor(y_in[5]), 1.0)
            sigma, steep = slope_of(edges)
            edge[0] = (edges * sigma * inside).astype(BF).astype(F32)
            edge[1] = steep * inside
            for m in range(6):
                for k in range(6):
                    at = slice(k * 128, k * 128 + 128)
                    mask = factor(x_in[m]) * factor(y_in[k])
                    value = acc[m, :, at]
                    sigma, steep = slope_of(value)
                    first = (value * sigma * mask).astype(BF)
                    act[m, :, at] = first
                    slope[m, :, at] = steep * mask
                    if 1 <= m < 5 and 1 <= k < 5:
                        total = total + first.astype(F32)
            total = total * (1.0 / 64.0)
        else:
            edge[2] = edges
            for m in range(6):
                d_join[m] = acc[m]
                if 1 <= m < 5:
                    for k in range(1, 5):
                        total = total + acc[m, :, k * 128 : k * 128 + 128]
        pooled[arr] = lax.dot_general(
            pool, total, NT, preferred_element_type=F32, precision=lax.Precision.HIGHEST
        )
    msg[...] = jnp.concatenate([pooled[0], pooled[1]], axis=1).astype(BF)


def split_two(value):
    high = value.astype(BF)
    low = (value - high.astype(F32)).astype(BF)
    return jnp.concatenate([high, low], axis=0)


def lane_tiles(sizes):
    count_x, count_y, count_z = sizes
    span, lift = 128 // count_y, 32 // count_y
    first = -(-(27 * span + lift) // 128)
    second = -(-(27 * span // count_z + lift // count_z) // 128)
    return first, second


def message_rows(sizes):
    i_mid, i_fine = 128 // sizes[0], 32 // sizes[0]
    tiles, _ = lane_tiles(sizes)
    used = tiles * i_mid + tiles * i_fine + 18 * i_fine
    return -(-used // 16) * 16


def final_rows(sizes):
    i_mid, i_fine = 128 // sizes[0], 32 // sizes[0]
    _, tiles = lane_tiles(sizes)
    used = tiles * i_mid + tiles * i_fine + 3 * (32 // (sizes[1] * sizes[2]))
    return -(-used // 8) * 8


def second(
    sizes, scale, place, recv, w_in, w_mid, w_lift, own, act, slope, d_join, edge,
    w_fine_in, w_fine_out,
    out, g_in, msg,
    raw, p3, c3, d3, e3, s2, c2, wp_in, wp_mid, bp_mid, b_in, lds, edge_rows,
    v_join, v_dz, acc, w_o, w_g, mbuf,
):
    count_x, count_y, count_z = sizes
    gx, gy, gz = place[0], place[1], place[2]
    rows = count_y * PITCH
    body_rows = slice(PITCH, PITCH + rows)
    deep_rows = slice(2 * PITCH, 2 * PITCH + rows)

    z_at = iota((PITCH, 128), 0)
    z_all = z_at + (gz * OWN - PAD)
    z_mask = ones_where((z_all >= 0) & (z_all < count_z * OWN))
    z_mask = jnp.concatenate([z_mask] * count_y, axis=0)
    own_mask = ones_where((z_at >= PAD) & (z_at < PAD + OWN))
    own_mask = jnp.concatenate([own_mask] * count_y, axis=0)

    for store, pads in ((p3, 1), (c3, 1), (d3, 1), (e3, 2), (c2, 1)):
        for plane in range(store.shape[0]):
            blank = jnp.zeros((pads * PITCH, store.shape[2]), BF)
            store[plane, 0 : pads * PITCH] = blank
            store[plane, pads * PITCH + rows : 2 * pads * PITCH + rows] = blank
    for a in range(3):
        for b in range(3):
            for c in range(3):
                tap = 9 * a + 3 * b + c
                side = slice(b * 128, b * 128 + 128)
                deep = slice(c * 128, c * 128 + 128)
                wp_in[a, c * 32 : c * 32 + 32, side] = w_in[tap]
                wp_mid[a, deep, side] = w_mid[tap]
                bp_mid[a, side, deep] = w_mid[26 - tap]
                b_in[3 * a + b, :, deep] = w_in[26 - tap]

    def inside(plane):
        at = gx + plane - PAD
        return (at >= 0) & (at < count_x), jnp.clip(at, 0, count_x - 1)

    def stacked(value):
        return jnp.concatenate([row_roll(value, 1), value, row_roll(value, -1)], axis=1).astype(BF)

    def unpack(plane, carry):
        ok, at = inside(plane)
        keep = ones_where(ok)
        parts = []
        for y in range(count_y):
            block = recv[at, y].astype(F32) * keep
            parts.append(block[:, :64])
            parts.append(block[:, 64:])
        whole = jnp.concatenate(parts, axis=0)
        raw[plane] = whole.astype(BF)
        p3[plane, body_rows, :] = stacked(whole[:, :32])
        return carry

    lax.fori_loop(0, 11, unpack, 0)

    def taps(store, first, pair, alone, product):
        total = None
        for a in range(3):
            both = product(store[first + a, 0 : rows + PITCH, :], pair(a))
            last = product(store[first + a, 2 * PITCH : 2 * PITCH + rows, :], alone(a))
            part = both[:rows, :128] + both[PITCH:, 128:] + last
            total = part if total is None else total + part
        return total

    def level_2(plane, carry):
        ok, _ = inside(plane)
        mask = z_mask * ones_where(ok)
        z_2 = taps(p3, plane - 1, lambda a: wp_in[a, :, :256], lambda a: wp_in[a, :, 256:], mm)
        sigma, steep = slope_of(z_2)
        s2[plane - 1] = steep * mask
        c3[plane - 1, body_rows, :] = stacked(z_2 * sigma * mask)
        return carry

    lax.fori_loop(1, 10, level_2, 0)
    lift_64 = jnp.concatenate([jnp.zeros((128, 32), F32), w_lift[...].astype(F32)], axis=1)
    lift_64 = lift_64.astype(BF)

    def level_3(plane, carry):
        ok, _ = inside(plane)
        mask = z_mask * ones_where(ok)
        z_3 = taps(c3, plane - 2, lambda a: wp_mid[a, :, :256], lambda a: wp_mid[a, :, 256:], mm)
        sigma, steep = slope_of(z_3)
        c2[plane - 2, body_rows, :] = (z_3 * sigma * mask).astype(BF)
        d_third = mm_nt(raw[plane], lift_64)
        d3[plane - 2, body_rows, :] = stacked(d_third * steep)
        return carry

    lax.fori_loop(2, 9, level_3, 0)

    def level_2_back(plane, carry):
        total = taps(d3, plane - 3, lambda a: bp_mid[a, :256], lambda a: bp_mid[a, 256:], mm_nt)
        e3[plane - 3, deep_rows, :] = stacked(total * s2[plane - 1])
        return carry

    lax.fori_loop(3, 8, level_2_back, 0)

    near = 3 * PITCH
    for x in range(3):
        d_pool = None
        for ab in range(9):
            start = pl.multiple_of((gy + ab % 3) * PITCH, PITCH)
            part = mm_nt(e3[x + ab // 3, pl.ds(start, near), :], b_in[ab])
            d_pool = part if d_pool is None else d_pool + part
        lifted = mm(c2[2 + x, pl.ds(pl.multiple_of(gy * PITCH, PITCH), near), :], w_lift[...])
        lds[x] = jnp.concatenate([lifted, d_pool], axis=1)

    span, lift_span = 128 // count_y, 32 // count_y
    tiles, _ = lane_tiles(sizes)
    lanes = tiles * 128
    col = iota((384, 3 * span), 1)
    share = iota((384, 3 * span), 0) == col // span * 128 + col % span + gy * span
    share = ones_where(share).astype(BF)

    def shifted(store, first, pads):
        parts = []
        for a in range(3):
            picked = mm(store[first + a], share)
            for b in range(3):
                start = (pads - 1 + b) * PITCH
                parts.append(picked[start : start + rows])
        parts.append(jnp.zeros((rows, lanes - 27 * span), F32))
        return jnp.concatenate(parts, axis=1).astype(BF)

    c1_own = (c3[4, body_rows, 128:256].astype(F32) * own_mask).astype(BF)
    c2_own = (c2[3, body_rows, :].astype(F32) * own_mask).astype(BF)
    raw_own = (raw[5].astype(F32) * own_mask[:, :64]).astype(BF)
    col = iota((64, lanes), 1) - 27 * span
    pick = (iota((64, lanes), 0) == col + 32 + gy * lift_span) & (col >= 0) & (col < lift_span)
    d_lift = mm(raw[5], ones_where(pick).astype(BF)).astype(BF)
    g_mid = (mm_tn(c1_own, shifted(d3, 2, 1)) + mm_tn(c2_own, d_lift)) * scale
    g_coarse = mm_tn(raw_own, shifted(e3, 1, 2)) * scale
    i_mid, i_fine = 128 // count_x, 32 // count_x
    for x in range(count_x):
        for tile in range(tiles):
            at = slice(tile * 128, tile * 128 + 128)
            to = tile * i_mid
            mbuf[x, to : to + i_mid, :] = g_mid[x * i_mid : (x + 1) * i_mid, at]
            to = tiles * i_mid + tile * i_fine
            mbuf[x, to : to + i_fine, :] = g_coarse[x * i_fine : (x + 1) * i_fine, at]

    forward_taps(w_fine_out, w_o)
    backward_taps(w_fine_in, w_g)
    lane = iota((32, 128), 1)
    up = ones_where(iota((PITCH, 128), 0) == iota((PITCH, 128), 1) // 4 + PAD).astype(BF)
    up = jnp.concatenate([up, up], axis=0)
    spread = {}
    for x in range(3):
        for y in range(3):
            spread[x, y] = mm_tn(split_two(lds[x, y * PITCH : y * PITCH + PITCH]), up)
    edge_rows[...] = jnp.zeros(edge_rows.shape, F32)
    for side in range(2):
        for x in range(3):
            for y in range(3):
                at = side * 9 + x * 3 + y
                z = y * PITCH + (PAD - 1 if side == 0 else PAD + OWN)
                edge_rows[at : at + 1, :] = lds[x, z : z + 1, :]
    cell = iota((24, 128), 1)
    x_at, y_at = cell % 64 // 8, cell % 8
    x_of = jnp.where(x_at == 0, 0, jnp.where(x_at == 5, 2, 1))
    y_of = jnp.where(y_at == 0, 0, jnp.where(y_at == 5, 2, 1))
    edge_up = iota((24, 128), 0) == cell // 64 * 9 + x_of * 3 + y_of
    edge_up = ones_where(edge_up & (x_at < 6) & (y_at < 6))
    edge_up = jnp.concatenate([edge_up, edge_up], axis=0).astype(BF)
    spread_e = mm_tn(split_two(edge_rows[...]), edge_up)
    join_e = (edge[0] + spread_e[:32]).astype(BF).astype(F32)
    dz_e = ((edge[2] + spread_e[32:] * (1.0 / 64.0)) * edge[1]).astype(BF).astype(F32)
    for m in range(6):
        for k in range(6):
            at = slice(k * 128, k * 128 + 128)
            over = spread[COARSE_OF[m], COARSE_OF[k]]
            join = (act[m, :, at].astype(F32) + over[:32]).astype(BF).astype(F32)
            v_join[m, :, at] = stacked_row(join, join_e, m * 8 + k, lane)
            dz = (d_join[m, :, at] + over[32:] * (1.0 / 64.0)) * slope[m, :, at]
            v_dz[m, :, at] = stacked_row(dz.astype(BF).astype(F32), dz_e, m * 8 + k, lane)
    for store, weight, result in ((v_join, w_o, out), (v_dz, w_g, g_in)):
        for x in range(4):
            acc[x] = jnp.zeros((32, 512), F32)
        for m in range(6):
            product = mm(weight[...], store[m])
            for a in range(3):
                x = m - a
                if 0 <= x < 4:
                    part = None
                    for b in range(3):
                        at = (3 * a + b) * 32
                        piece = product[at : at + 32, b * 128 : b * 128 + 512]
                        part = piece if part is None else part + piece
                    acc[x] = acc[x] + part
        for x in range(4):
            for y in range(4):
                result[x, y] = acc[x, :, y * 128 : y * 128 + 128].astype(BF)
    flat = [
        [jnp.concatenate([own[arr, x, y] for y in range(4)], axis=1) for x in range(4)]
        for arr in range(2)
    ]
    base = tiles * (i_mid + i_fine)
    for ab in range(9):
        a, b = ab // 3, ab % 3
        at = slice(b * 128, b * 128 + 512)
        total_o = None
        total_i = None
        for x in range(4):
            part_o = mm_nt(v_join[x + a, :, at], flat[1][x])
            part_i = mm_nt(flat[0][x], v_dz[x + a, :, at])
            total_o = part_o if total_o is None else total_o + part_o
            total_i = part_i if total_i is None else total_i + part_i
        by_tap = [total_o[c * 32 : c * 32 + 32] for c in range(3)]
        both = (jnp.concatenate(by_tap, axis=1) * scale, total_i * scale)
        for kind in range(2):
            to = base + (kind * 9 + ab) * i_fine
            for x in range(count_x):
                mbuf[x, to : to + i_fine, 0:96] = both[kind][x * i_fine : (x + 1) * i_fine]
                mbuf[x, to : to + i_fine, 96:128] = jnp.zeros((i_fine, 32), F32)
    used = base + 18 * i_fine
    for x in range(count_x):
        if used < mbuf.shape[1]:
            mbuf[x, used:, :] = jnp.zeros((mbuf.shape[1] - used, 128), F32)
        msg[x] = mbuf[x].astype(BF)


def gz_perm(sizes):
    count_x, count_y, count_z = sizes
    tiles, parts = lane_tiles(sizes)
    span, lift = 128 // count_y, 32 // count_y
    each, lift_each = span // count_z, lift // count_z
    perm = np.zeros((tiles * 128, count_z * parts * 128), np.float32)
    for z in range(count_z):
        base = z * parts * 128
        for tap in range(27):
            for o in range(each):
                perm[tap * span + z * each + o, base + tap * each + o] = 1
        for o in range(lift_each):
            perm[27 * span + z * lift_each + o, base + 27 * each + o] = 1
    return jnp.asarray(perm, BF)


def split_three(value):
    high = value.astype(BF)
    rest = value - high.astype(F32)
    mid = rest.astype(BF)
    low = (rest - mid.astype(F32)).astype(BF)
    return high, mid, low


def regroup(sizes, place, recv, perm, out, buf):
    count_x, count_y, count_z = sizes
    gy = place[1]
    i_mid, i_fine = 128 // count_x, 32 // count_x
    tiles, parts = lane_tiles(sizes)
    total = recv[0].astype(F32)
    for x in range(1, count_x):
        total = total + recv[x].astype(F32)
    base = tiles * i_mid
    mid = jnp.concatenate([total[t * i_mid : (t + 1) * i_mid] for t in range(tiles)], axis=1)
    low = [total[base + t * i_fine : base + (t + 1) * i_fine] for t in range(tiles)]
    low = jnp.concatenate(low, axis=1)
    count = i_mid + i_fine
    padded = -(-count // 16) * 16
    blank = jnp.zeros((padded - count, tiles * 128), F32)
    coarse = jnp.concatenate([mid, low, blank], axis=0)
    moved = None
    for part in split_three(coarse):
        term = mm(part, perm[...])
        moved = term if moved is None else moved + term
    base = tiles * (i_mid + i_fine)
    fine = total[base : base + 18 * i_fine]
    fine = jnp.concatenate([fine, jnp.zeros((128 - 18 * i_fine, 128), F32)], axis=0)
    buf[...] = jnp.transpose(fine)
    each = 32 // (count_y * count_z)
    fine_at = parts * count
    for y in range(count_y):
        keep = ones_where(gy == y)
        for z in range(count_z):
            at = y * count_z + z
            for t in range(parts):
                piece = moved[:count, (z * parts + t) * 128 : (z * parts + t + 1) * 128] * keep
                out[at, t * count : (t + 1) * count, :] = piece
            for c in range(3):
                to = fine_at + c * each
                source = c * 32 + at * each
                out[at, to : to + each, :] = buf[source : source + each, :]
            used = fine_at + 3 * each
            if used < out.shape[1]:
                out[at, used:, :] = jnp.zeros((out.shape[1] - used, 128), F32)


def finish(sizes, recv, fine_in, coarse_in, coarse_mid, lift, fine_out):
    count_x, count_y, count_z = sizes
    i_mid, i_fine = 128 // count_x, 32 // count_x
    _, parts = lane_tiles(sizes)
    total = recv[0]
    for at in range(1, count_y * count_z):
        total = total + recv[at]
    count = i_mid + i_fine
    wide = jnp.concatenate([total[t * count : (t + 1) * count] for t in range(parts)], axis=1)
    each = 128 // (count_y * count_z)
    for tap in range(27):
        piece = wide[:, tap * each : (tap + 1) * each]
        coarse_mid[26 - tap] = piece[:i_mid]
        coarse_in[26 - tap] = piece[i_mid:]
    lift_each = 32 // (count_y * count_z)
    lift[...] = wide[:i_mid, 27 * each : 27 * each + lift_each]
    base = parts * count
    rest = total[base : base + 3 * lift_each]
    rest = jnp.concatenate([rest, jnp.zeros((128 - 3 * lift_each, 128), F32)], axis=0)
    rest = jnp.transpose(rest)
    for ab in range(9):
        for c in range(3):
            side = slice(c * lift_each, (c + 1) * lift_each)
            tap = 3 * ab + c
            fine_out[tap] = rest[ab * i_fine : (ab + 1) * i_fine, side]
            fine_in[26 - tap] = rest[(9 + ab) * i_fine : (10 + ab) * i_fine, side]


def from_below(value, axis):
    count = lax.axis_size(axis)
    return lax.ppermute(value, axis, [(i, i + 1) for i in range(count - 1)])


def from_above(value, axis):
    count = lax.axis_size(axis)
    return lax.ppermute(value, axis, [(i + 1, i) for i in range(count - 1)])


def shape_of(shape, dtype):
    return jax.ShapeDtypeStruct(shape, dtype)


def shards(features, cotangent, w_fine_in, w_coarse_in, w_coarse_mid, w_lift, w_fine_out):
    sizes = (lax.axis_size(GX), lax.axis_size("gy"), lax.axis_size("gz"))
    count_x, count_y, count_z = sizes
    cells = count_x * count_y * count_z * 4 * 4 * 128
    scale = 1.0 / math.sqrt(cells)
    place = jnp.stack([lax.axis_index(GX), lax.axis_index("gy"), lax.axis_index("gz")])
    place = place.astype(jnp.int32)

    own = jnp.stack([features, cotangent]).transpose(0, 2, 3, 1, 4)
    xlo = from_below(own[:, 2:4], GX)
    xhi = from_above(own[:, 0:2], GX)
    y_tail = jnp.concatenate([xlo[:, :, 2:4], own[:, :, 2:4], xhi[:, :, 2:4]], axis=1)
    y_head = jnp.concatenate([xlo[:, :, 0:2], own[:, :, 0:2], xhi[:, :, 0:2]], axis=1)
    ylo = from_below(y_tail, "gy")
    yhi = from_above(y_head, "gy")
    face = call(z_faces, shape_of((2, 2, 32, 128), BF), [], 5, False, 4)(own, xlo, xhi, ylo, yhi)
    face_l = from_below(face, "gz")
    face_r = from_above(face, "gz")
    taps = pltpu.VMEM((288, 96), BF)
    act, slope, d_join, edge, msg = call(
        functools.partial(fine_first, sizes),
        (
            shape_of((6, 32, 768), BF),
            shape_of((6, 32, 768), F32),
            shape_of((6, 32, 768), F32),
            shape_of((3, 32, 128), F32),
            shape_of((32, 64), BF),
        ),
        [pltpu.VMEM((6, 32, 768), F32), pltpu.VMEM((96, 1024), BF), taps, taps],
        11,
        True,
        10,
    )(place, own, xlo, xhi, ylo, yhi, face, face_l, face_r, w_fine_in, w_fine_out)

    z_lo = from_below(msg[24:32], "gz")
    z_hi = from_above(msg[0:8], "gz")
    window = jnp.concatenate(
        [z_lo[8 - PAD :], msg, z_hi[:PAD], jnp.zeros((PITCH - OWN - 2 * PAD, 64), BF)], axis=0
    )
    packed = jnp.concatenate([window[:24], window[24:]], axis=1)
    recv = lax.all_to_all(
        jnp.broadcast_to(packed[None], (count_x * count_y, 24, 128)),
        GX + ("gy",),
        split_axis=0,
        concat_axis=0,
        tiled=True,
    ).reshape(count_x, count_y, 24, 128)

    rows = count_y * PITCH
    wide = rows + 2 * PITCH
    out, grad_input, msg = call(
        functools.partial(second, sizes, scale),
        (
            shape_of((4, 4, 32, 128), BF),
            shape_of((4, 4, 32, 128), BF),
            shape_of((count_x, message_rows(sizes), 128), BF),
        ),
        [
            pltpu.VMEM((11, rows, 64), BF),
            pltpu.VMEM((11, wide, 96), BF),
            pltpu.VMEM((9, wide, 384), BF),
            pltpu.VMEM((7, wide, 384), BF),
            pltpu.VMEM((5, wide + 2 * PITCH, 384), BF),
            pltpu.VMEM((9, rows, 128), F32),
            pltpu.VMEM((7, wide, 128), BF),
            pltpu.VMEM((3, 96, 384), BF),
            pltpu.VMEM((3, 384, 384), BF),
            pltpu.VMEM((3, 384, 384), BF),
            pltpu.VMEM((9, 32, 384), BF),
            pltpu.VMEM((3, 3 * PITCH, 64), F32),
            pltpu.VMEM((24, 64), F32),
            pltpu.VMEM((6, 96, 768), BF),
            pltpu.VMEM((6, 96, 768), BF),
            pltpu.VMEM((4, 32, 512), F32),
            taps,
            taps,
            pltpu.VMEM((count_x, message_rows(sizes), 128), F32),
        ],
        12,
        True,
        34,
    )(
        place, recv, w_coarse_in, w_coarse_mid, w_lift, own, act, slope, d_join, edge,
        w_fine_in, w_fine_out,
    )
    out = out.transpose(2, 0, 1, 3)
    grad_input = grad_input.transpose(2, 0, 1, 3)

    msg = lax.all_to_all(msg, GX, split_axis=0, concat_axis=0, tiled=True)
    msg = call(
        functools.partial(regroup, sizes),
        shape_of((count_y * count_z, final_rows(sizes), 128), F32),
        [pltpu.VMEM((128, 128), F32)],
        3,
        True,
        6,
    )(place, msg, gz_perm(sizes))
    msg = lax.all_to_all(msg, ("gy", "gz"), split_axis=0, concat_axis=0, tiled=True)
    i_mid, i_fine = 128 // count_x, 32 // count_x
    o_mid, o_fine = 128 // (count_y * count_z), 32 // (count_y * count_z)
    grads = call(
        functools.partial(finish, sizes),
        (
            shape_of((27, i_fine, o_fine), F32),
            shape_of((27, i_fine, o_mid), F32),
            shape_of((27, i_mid, o_mid), F32),
            shape_of((i_mid, o_fine), F32),
            shape_of((27, i_fine, o_fine), F32),
        ),
        [],
        1,
        False,
        6,
        False,
    )(msg)
    return (out, grad_input, *grads)


def solution(mesh):
    split = Mesh(
        mesh.devices.reshape(mesh.shape["gx"] // 2, 2, mesh.shape["gy"], mesh.shape["gz"]),
        ("gx_0", "gx_1", "gy", "gz"),
    )
    return jax.shard_map(
        shards,
        mesh=split,
        in_specs=(P(None, GX, "gy", "gz"), P(None, GX, "gy", "gz"), P(), P(), P(), P(), P()),
        out_specs=(
            P(None, GX, "gy", "gz"),
            P(None, GX, "gy", "gz"),
            P(None, GX, ("gy", "gz")),
            P(None, GX, ("gy", "gz")),
            P(None, GX, ("gy", "gz")),
            P(GX, ("gy", "gz")),
            P(None, GX, ("gy", "gz")),
        ),
        check_vma=False,
    )
```

```python
import functools
import math

import jax
import jax.numpy as jnp
import numpy as np
from jax import lax
from jax.experimental import pallas as pl
from jax.experimental.pallas import tpu as pltpu
from jax.sharding import Mesh
from jax.sharding import PartitionSpec as P

GX = ("gx_0", "gx_1")
GY = ("gy_0", "gy_1")
INTERPRET = False
BF = jnp.bfloat16
F32 = jnp.float32
PAD = 5
OWN = 32
PITCH = 48
NT = (((1,), (1,)), ((), ()))
TN = (((0,), (0,)), ((), ()))
COARSE_OF = (0, 1, 1, 1, 1, 2)


def mm(lhs, rhs):
    return jnp.dot(lhs, rhs, preferred_element_type=F32)


def mm_nt(lhs, rhs):
    return lax.dot_general(lhs, rhs, NT, preferred_element_type=F32)


def mm_tn(lhs, rhs):
    return lax.dot_general(lhs, rhs, TN, preferred_element_type=F32)


def lane_roll(value, shift):
    return pltpu.roll(value, shift % value.shape[1], 1)


def row_roll(value, shift):
    return pltpu.roll(value, shift % value.shape[0], 0)


def call(body, out_shape, scratch, n_in, smem_first, megabytes, keep_out=True, in_hbm=0):
    spec = [pl.BlockSpec(memory_space=pltpu.VMEM)] * n_in
    if smem_first:
        spec[0] = pl.BlockSpec(memory_space=pltpu.SMEM)
    spec = spec + [pl.BlockSpec(memory_space=pl.ANY)] * in_hbm
    out_spec = pl.BlockSpec(memory_space=pltpu.VMEM) if keep_out else pl.BlockSpec()
    return pl.pallas_call(
        body,
        out_shape=out_shape,
        in_specs=spec,
        out_specs=jax.tree.map(lambda _: out_spec, out_shape),
        scratch_shapes=scratch,
        compiler_params=pltpu.CompilerParams(vmem_limit_bytes=megabytes * 1024 * 1024),
        interpret=INTERPRET,
    )


def rows_of(own, xlo, xhi, ylo, yhi):
    def row(arr, xi, yi):
        if yi < 2:
            return ylo[arr, xi, yi]
        if yi >= 6:
            return yhi[arr, xi, yi - 6]
        if xi < 2:
            return xlo[arr, xi, yi - 2]
        if xi >= 6:
            return xhi[arr, xi - 6, yi - 2]
        return own[arr, xi - 2, yi - 2]

    return row


def iota(shape, dim):
    return lax.broadcasted_iota(jnp.int32, shape, dim)


def ones_where(flag):
    return jnp.where(flag, 1.0, 0.0)


def z_faces(own, xlo, xhi, ylo, yhi, out):
    row = rows_of(own, xlo, xhi, ylo, yhi)
    lane = iota((32, 128), 1)
    column = iota((256, 256), 1)
    source = jnp.where(column < 128, 0, 1)
    source = jnp.where(column % 128 < 64, source, 3 - source)
    perm = ones_where(iota((256, 256), 0) == column % 64 * 4 + source).astype(BF)
    for arr in range(2):
        halves = []
        for half in range(2):
            gathered = jnp.zeros((32, 128), F32)
            for at in range(32):
                cell = half * 32 + at
                value = row(arr, cell // 8, cell % 8).astype(F32)
                moved = lane_roll(value, 4 * at + 2)
                here = (lane >= 4 * at) & (lane < 4 * at + 4)
                gathered = jnp.where(here, moved, gathered)
            halves.append(gathered.astype(BF))
        tiles = mm(jnp.concatenate(halves, axis=1), perm).astype(BF)
        out[arr, 0] = tiles[:, :128]
        out[arr, 1] = tiles[:, 128:]


def stacked_row(value, edge, cell, lane):
    before = jnp.where(lane == 0, lane_roll(edge, -cell), lane_roll(value, 1))
    after = jnp.where(lane == 127, lane_roll(edge, 63 - cell), lane_roll(value, -1))
    return jnp.concatenate([before, value, after], axis=0).astype(BF)


def edge_sum(weight, tile):
    product = mm(weight, tile)
    total = None
    for ab in range(9):
        part = lane_roll(product[ab * 32 : ab * 32 + 32], -(ab // 3 * 8 + ab % 3))
        total = part if total is None else total + part
    return total


def slope_of(value):
    sigma = jax.nn.sigmoid(value)
    return sigma, sigma * (1.0 + value * (1.0 - sigma))


def forward_taps(weight, store):
    same = ones_where(iota((32, 32), 0) == iota((32, 32), 1)).astype(BF)
    for ab in range(9):
        stack = jnp.concatenate([weight[3 * ab + c] for c in range(3)], axis=0)
        store[ab * 32 : ab * 32 + 32, :] = mm_nt(same, stack).astype(BF)


def backward_taps(weight, store):
    for ab in range(9):
        stack = [weight[26 - 3 * ab - c].astype(F32) for c in range(3)]
        store[ab * 32 : ab * 32 + 32, :] = jnp.concatenate(stack, axis=1).astype(BF)


def fine_first(
    sizes, place, own, xlo, xhi, ylo, yhi, face, face_l, face_r, w_fine_in, w_fine_out,
    keep, msg, acc, vbuf, w_z, w_d,
):
    count_x, count_y, count_z = sizes
    gx, gy, gz = place[0], place[1], place[2]
    row = rows_of(own, xlo, xhi, ylo, yhi)
    lane = iota((32, 128), 1)
    lower = lane < 64
    x_in = [gx > 0, None, None, None, None, gx < count_x - 1]
    y_in = [gy > 0, None, None, None, None, gy < count_y - 1]
    forward_taps(w_fine_in, w_z)
    backward_taps(w_fine_out, w_d)

    def factor(flag):
        return 1.0 if flag is None else jnp.where(flag, 1.0, 0.0)

    pooled = {}
    pool = ones_where(iota((32, 128), 1) // 4 == iota((32, 128), 0))
    for arr, weight in ((0, w_z), (1, w_d)):
        tile_a, tile_b = face[arr, 0].astype(F32), face[arr, 1].astype(F32)
        left_a, left_b = face_l[arr, 0].astype(F32), face_l[arr, 1].astype(F32)
        right_a, right_b = face_r[arr, 0].astype(F32), face_r[arr, 1].astype(F32)
        swapped = lane_roll(tile_b, 64)
        edge_0 = jnp.where(lower, left_a, swapped)
        edge_1 = jnp.where(lower, left_b, right_b)
        edge_2 = jnp.where(lower, swapped, right_a)
        edges = edge_sum(weight[...], jnp.concatenate([edge_0, edge_1, edge_2], axis=0).astype(BF))
        for m in range(6):
            acc[m] = jnp.zeros((32, 768), F32)
        for xi in range(8):
            for yi in range(8):
                value = row(arr, xi, yi).astype(F32)
                vbuf[:, yi * 128 : yi * 128 + 128] = stacked_row(value, edge_1, xi * 8 + yi, lane)
            product = mm(weight[...], vbuf[...])
            for a in range(3):
                m = xi - a
                if 0 <= m < 6:
                    part = None
                    for b in range(3):
                        at = (3 * a + b) * 32
                        piece = product[at : at + 32, b * 128 : b * 128 + 768]
                        part = piece if part is None else part + piece
                    acc[m] = acc[m] + part
        total = jnp.zeros((32, 128), F32)
        if arr == 0:
            x_at = lane % 64 // 8
            y_at = lane % 8
            inside = jnp.where(lower, factor(gz > 0), factor(gz < count_z - 1))
            inside = inside * jnp.where(x_at == 0, factor(x_in[0]), 1.0)
            inside = inside * jnp.where(x_at == 5, factor(x_in[5]), 1.0)
            inside = inside * jnp.where(y_at == 0, factor(y_in[0]), 1.0)
            inside = inside * jnp.where(y_at == 5, factor(y_in[5]), 1.0)
            sigma, steep = slope_of(edges)
            keep[18, :, 0:128] = (edges * sigma * inside).astype(BF).astype(F32)
            keep[18, :, 128:256] = steep * inside
            for m in range(6):
                for k in range(6):
                    at = slice(k * 128, k * 128 + 128)
                    mask = factor(x_in[m]) * factor(y_in[k])
                    value = acc[m, :, at]
                    sigma, steep = slope_of(value)
                    first = (value * sigma * mask).astype(BF)
                    keep[m, :, at] = first.astype(F32)
                    keep[6 + m, :, at] = steep * mask
                    if 1 <= m < 5 and 1 <= k < 5:
                        total = total + first.astype(F32)
            total = total * (1.0 / 64.0)
        else:
            keep[18, :, 256:384] = edges
            for m in range(6):
                keep[12 + m] = acc[m]
                if 1 <= m < 5:
                    for k in range(1, 5):
                        total = total + acc[m, :, k * 128 : k * 128 + 128]
        pooled[arr] = lax.dot_general(
            pool, total, NT, preferred_element_type=F32, precision=lax.Precision.HIGHEST
        )
    msg[...] = jnp.concatenate([pooled[0], pooled[1]], axis=1).astype(BF)


def split_two(value):
    high = value.astype(BF)
    low = (value - high.astype(F32)).astype(BF)
    return jnp.concatenate([high, low], axis=0)


def lane_tiles(sizes):
    count_x, count_y, count_z = sizes
    span, lift = 128 // count_y, 32 // count_y
    first = -(-(27 * span + lift) // 128)
    second = -(-(span // count_z * 32) // 128)
    return first, second


def message_rows(sizes):
    i_mid, i_fine = 128 // sizes[0], 32 // sizes[0]
    tiles, _ = lane_tiles(sizes)
    used = tiles * i_mid + tiles * i_fine + 18 * i_fine
    return -(-used // 16) * 16


def final_rows(sizes):
    i_mid, i_fine = 128 // sizes[0], 32 // sizes[0]
    _, tiles = lane_tiles(sizes)
    used = tiles * i_mid + tiles * i_fine + 3 * (32 // (sizes[1] * sizes[2]))
    return -(-used // 16) * 16


def second(
    sizes, scale, place, recv, recv_far, own, keep,
    w_in_hbm, w_mid_hbm, w_lift_hbm, w_fine_in_hbm, w_fine_out_hbm,
    out, g_in, msg,
    raw, p3, c3, d3, e3, s2, c2, wp_in, wp_mid, bp_mid, b_in, lds, edge_rows,
    v_join, v_dz, acc, w_o, w_g, mbuf, w_in, w_mid, w_lift, w_fine_in, w_fine_out, arrived,
):
    count_x, count_y, count_z = sizes
    loads = [
        pltpu.make_async_copy(source, target, arrived.at[at])
        for at, (source, target) in enumerate(
            (
                (w_in_hbm, w_in),
                (w_mid_hbm, w_mid),
                (w_lift_hbm, w_lift),
                (w_fine_in_hbm, w_fine_in),
                (w_fine_out_hbm, w_fine_out),
            )
        )
    ]
    for load in loads:
        load.start()
    gx, gy, gz = place[0], place[1], place[2]
    rows = count_y * PITCH
    body_rows = slice(PITCH, PITCH + rows)
    deep_rows = slice(2 * PITCH, 2 * PITCH + rows)

    z_at = iota((PITCH, 128), 0)
    z_all = z_at + (gz * OWN - PAD)
    z_mask = ones_where((z_all >= 0) & (z_all < count_z * OWN))
    z_mask = jnp.concatenate([z_mask] * count_y, axis=0)
    own_mask = ones_where((z_at >= PAD) & (z_at < PAD + OWN))
    own_mask = jnp.concatenate([own_mask] * count_y, axis=0)

    for store, pads in ((p3, 1), (c3, 1), (d3, 1), (e3, 2), (c2, 1)):
        for plane in range(store.shape[0]):
            blank = jnp.zeros((pads * PITCH, store.shape[2]), BF)
            store[plane, 0 : pads * PITCH] = blank
            store[plane, pads * PITCH + rows : 2 * pads * PITCH + rows] = blank
    def inside(plane):
        at = gx + plane - PAD
        return (at >= 0) & (at < count_x), jnp.clip(at, 0, count_x - 1)

    def stacked(value):
        return jnp.concatenate([row_roll(value, 1), value, row_roll(value, -1)], axis=1).astype(BF)

    def unpack(plane, carry):
        ok, at = inside(plane)
        valid = ones_where(ok)
        parts = []
        for y in range(count_y):
            near_by = lax.rem(gy, 2) == y % 2
            block = jnp.where(near_by, recv[at, y // 2], recv_far[at, y // 2]).astype(F32) * valid
            parts.append(block[:, :64])
            parts.append(block[:, 64:])
        whole = jnp.concatenate(parts, axis=0)
        raw[plane] = whole.astype(BF)
        first = whole[:, :32]
        around = [row_roll(first, 1), first, row_roll(first, -1), jnp.zeros((rows, 32), F32)]
        p3[plane, body_rows, :] = jnp.concatenate(around, axis=1).astype(BF)
        return carry

    lax.fori_loop(0, 11, unpack, 0)

    for load in loads:
        load.wait()
    wp_in[...] = jnp.zeros(wp_in.shape, BF)
    for a in range(3):
        for b in range(3):
            for c in range(3):
                tap = 9 * a + 3 * b + c
                side = slice(b * 128, b * 128 + 128)
                deep = slice(a * 384 + c * 128, a * 384 + c * 128 + 128)
                wp_in[a * 128 + c * 32 : a * 128 + c * 32 + 32, side] = w_in[tap]
                wp_mid[deep, side] = w_mid[tap]
                bp_mid[side, deep] = w_mid[26 - tap]
                b_in[3 * a + b, :, c * 128 : c * 128 + 128] = w_in[26 - tap]

    def taps(store, first, pair, alone, product):
        top = [store[first + a, 0 : rows + PITCH, :] for a in range(3)]
        end = [store[first + a, 2 * PITCH : 2 * PITCH + rows, :] for a in range(3)]
        both = product(jnp.concatenate(top, axis=1), pair)
        last = product(jnp.concatenate(end, axis=1), alone)
        return both[:rows, :128] + both[PITCH:, 128:] + last

    def level_2(plane, carry):
        ok, _ = inside(plane)
        mask = z_mask * ones_where(ok)
        z_2 = taps(p3, plane - 1, wp_in[:, :256], wp_in[:, 256:], mm)
        sigma, steep = slope_of(z_2)
        s2[plane - 1] = steep * mask
        c3[plane - 1, body_rows, :] = stacked(z_2 * sigma * mask)
        return carry

    lax.fori_loop(1, 10, level_2, 0)
    lift_64 = jnp.concatenate([jnp.zeros((32, 128), BF), w_lift[...]], axis=0)

    def level_3(plane, carry):
        ok, _ = inside(plane)
        mask = z_mask * ones_where(ok)
        z_3 = taps(c3, plane - 2, wp_mid[:, :256], wp_mid[:, 256:], mm)
        sigma, steep = slope_of(z_3)
        c2[plane - 2, body_rows, :] = (z_3 * sigma * mask).astype(BF)
        d_third = mm(raw[plane], lift_64)
        d3[plane - 2, body_rows, :] = stacked(d_third * steep)
        return carry

    lax.fori_loop(2, 9, level_3, 0)

    def level_2_back(plane, carry):
        total = taps(d3, plane - 3, bp_mid[:256, :], bp_mid[256:, :], mm_nt)
        e3[plane - 3, deep_rows, :] = stacked(total * s2[plane - 1])
        return carry

    lax.fori_loop(3, 8, level_2_back, 0)

    near = 3 * PITCH
    for x in range(3):
        d_pool = None
        for ab in range(9):
            start = pl.multiple_of((gy + ab % 3) * PITCH, PITCH)
            part = mm_nt(e3[x + ab // 3, pl.ds(start, near), :], b_in[ab])
            d_pool = part if d_pool is None else d_pool + part
        lifted = mm_nt(c2[2 + x, pl.ds(pl.multiple_of(gy * PITCH, PITCH), near), :], w_lift[...])
        lds[x] = jnp.concatenate([lifted, d_pool], axis=1)

    span, lift_span = 128 // count_y, 32 // count_y
    tiles, _ = lane_tiles(sizes)
    lanes = tiles * 128
    col = iota((384, 3 * span), 1)
    share = iota((384, 3 * span), 0) == col // span * 128 + col % span + gy * span
    share = ones_where(share).astype(BF)

    def shifted(store, first, pads):
        parts = []
        for a in range(3):
            picked = mm(store[first + a], share)
            for b in range(3):
                start = (pads - 1 + b) * PITCH
                parts.append(picked[start : start + rows])
        parts.append(jnp.zeros((rows, lanes - 27 * span), F32))
        return jnp.concatenate(parts, axis=1).astype(BF)

    c1_own = (c3[4, body_rows, 128:256].astype(F32) * own_mask).astype(BF)
    c2_own = (c2[3, body_rows, :].astype(F32) * own_mask).astype(BF)
    raw_own = (raw[5].astype(F32) * own_mask[:, :64]).astype(BF)
    col = iota((64, lanes), 1) - 27 * span
    pick = (iota((64, lanes), 0) == col + 32 + gy * lift_span) & (col >= 0) & (col < lift_span)
    d_lift = mm(raw[5], ones_where(pick).astype(BF)).astype(BF)
    g_mid = (mm_tn(c1_own, shifted(d3, 2, 1)) + mm_tn(c2_own, d_lift)) * scale
    g_coarse = mm_tn(raw_own, shifted(e3, 1, 2)) * scale
    i_mid, i_fine = 128 // count_x, 32 // count_x
    for x in range(count_x):
        for tile in range(tiles):
            at = slice(tile * 128, tile * 128 + 128)
            to = tile * i_mid
            mbuf[x, to : to + i_mid, :] = g_mid[x * i_mid : (x + 1) * i_mid, at]
            to = tiles * i_mid + tile * i_fine
            mbuf[x, to : to + i_fine, :] = g_coarse[x * i_fine : (x + 1) * i_fine, at]

    forward_taps(w_fine_out, w_o)
    backward_taps(w_fine_in, w_g)
    lane = iota((32, 128), 1)
    up = ones_where(iota((PITCH, 128), 0) == iota((PITCH, 128), 1) // 4 + PAD).astype(BF)
    up = jnp.concatenate([up, up], axis=0)
    spread = {}
    for x in range(3):
        for y in range(3):
            spread[x, y] = mm_tn(split_two(lds[x, y * PITCH : y * PITCH + PITCH]), up)
    edge_rows[...] = jnp.zeros(edge_rows.shape, F32)
    for side in range(2):
        for x in range(3):
            for y in range(3):
                at = side * 9 + x * 3 + y
                z = y * PITCH + (PAD - 1 if side == 0 else PAD + OWN)
                edge_rows[at : at + 1, :] = lds[x, z : z + 1, :]
    cell = iota((24, 128), 1)
    x_at, y_at = cell % 64 // 8, cell % 8
    x_of = jnp.where(x_at == 0, 0, jnp.where(x_at == 5, 2, 1))
    y_of = jnp.where(y_at == 0, 0, jnp.where(y_at == 5, 2, 1))
    edge_up = iota((24, 128), 0) == cell // 64 * 9 + x_of * 3 + y_of
    edge_up = ones_where(edge_up & (x_at < 6) & (y_at < 6))
    edge_up = jnp.concatenate([edge_up, edge_up], axis=0).astype(BF)
    spread_e = mm_tn(split_two(edge_rows[...]), edge_up)
    join_e = (keep[18, :, 0:128] + spread_e[:32]).astype(BF).astype(F32)
    dz_e = (keep[18, :, 256:384] + spread_e[32:] * (1.0 / 64.0)) * keep[18, :, 128:256]
    dz_e = dz_e.astype(BF).astype(F32)
    for m in range(6):
        for k in range(6):
            at = slice(k * 128, k * 128 + 128)
            over = spread[COARSE_OF[m], COARSE_OF[k]]
            join = (keep[m, :, at] + over[:32]).astype(BF).astype(F32)
            v_join[m, :, at] = stacked_row(join, join_e, m * 8 + k, lane)
            dz = (keep[12 + m, :, at] + over[32:] * (1.0 / 64.0)) * keep[6 + m, :, at]
            v_dz[m, :, at] = stacked_row(dz.astype(BF).astype(F32), dz_e, m * 8 + k, lane)
    for store, weight, result in ((v_join, w_o, out), (v_dz, w_g, g_in)):
        for x in range(4):
            acc[x] = jnp.zeros((32, 512), F32)
        for m in range(6):
            product = mm(weight[...], store[m])
            for a in range(3):
                x = m - a
                if 0 <= x < 4:
                    part = None
                    for b in range(3):
                        at = (3 * a + b) * 32
                        piece = product[at : at + 32, b * 128 : b * 128 + 512]
                        part = piece if part is None else part + piece
                    acc[x] = acc[x] + part
        for x in range(4):
            for y in range(4):
                result[x, y] = acc[x, :, y * 128 : y * 128 + 128].astype(BF)
    flat = [
        [jnp.concatenate([own[arr, x, y] for y in range(4)], axis=1) for x in range(4)]
        for arr in range(2)
    ]
    base = tiles * (i_mid + i_fine)
    for ab in range(9):
        a, b = ab // 3, ab % 3
        at = slice(b * 128, b * 128 + 512)
        total_o = None
        total_i = None
        for x in range(4):
            part_o = mm_nt(v_join[x + a, :, at], flat[1][x])
            part_i = mm_nt(flat[0][x], v_dz[x + a, :, at])
            total_o = part_o if total_o is None else total_o + part_o
            total_i = part_i if total_i is None else total_i + part_i
        by_tap = [total_o[c * 32 : c * 32 + 32] for c in range(3)]
        both = (jnp.concatenate(by_tap, axis=1) * scale, total_i * scale)
        for kind in range(2):
            to = base + (kind * 9 + ab) * i_fine
            for x in range(count_x):
                mbuf[x, to : to + i_fine, 0:96] = both[kind][x * i_fine : (x + 1) * i_fine]
                mbuf[x, to : to + i_fine, 96:128] = jnp.zeros((i_fine, 32), F32)
    used = base + 18 * i_fine
    for x in range(count_x):
        if used < mbuf.shape[1]:
            mbuf[x, used:, :] = jnp.zeros((mbuf.shape[1] - used, 128), F32)
        msg[x] = mbuf[x].astype(BF)


def gz_perm(sizes):
    count_x, count_y, count_z = sizes
    tiles, parts = lane_tiles(sizes)
    span, lift = 128 // count_y, 32 // count_y
    each, lift_each = span // count_z, lift // count_z
    perm = np.zeros((tiles * 128, count_z * parts * 128), np.float32)
    for z in range(count_z):
        base = z * parts * 128
        for tap in range(27):
            for o in range(each):
                perm[tap * span + z * each + o, base + o * 32 + 26 - tap] = 1
        for o in range(lift_each):
            perm[27 * span + z * lift_each + o, base + o * 32 + 27] = 1
    return jnp.asarray(perm, BF)


def split_three(value):
    high = value.astype(BF)
    rest = value - high.astype(F32)
    mid = rest.astype(BF)
    low = (rest - mid.astype(F32)).astype(BF)
    return high, mid, low


def regroup(sizes, place, recv, perm, out, buf, line):
    count_x, count_y, count_z = sizes
    gy = place[1]
    i_mid, i_fine = 128 // count_x, 32 // count_x
    tiles, parts = lane_tiles(sizes)
    total = recv[0].astype(F32)
    for x in range(1, count_x):
        total = total + recv[x].astype(F32)
    base = tiles * i_mid
    mid = jnp.concatenate([total[t * i_mid : (t + 1) * i_mid] for t in range(tiles)], axis=1)
    low = [total[base + t * i_fine : base + (t + 1) * i_fine] for t in range(tiles)]
    low = jnp.concatenate(low, axis=1)
    count = i_mid + i_fine
    padded = -(-count // 16) * 16
    blank = jnp.zeros((padded - count, tiles * 128), F32)
    coarse = jnp.concatenate([mid, low, blank], axis=0)
    moved = None
    for part in split_three(coarse):
        term = mm(part, perm[...])
        moved = term if moved is None else moved + term
    base = tiles * (i_mid + i_fine)
    fine = total[base : base + 18 * i_fine]
    fine = jnp.concatenate([fine, jnp.zeros((128 - 18 * i_fine, 128), F32)], axis=0)
    buf[...] = jnp.transpose(fine)
    each = 32 // (count_y * count_z)
    fine_at = parts * count
    line[...] = jnp.zeros(line.shape, F32)
    for y in range(count_y):
        own_y = ones_where(gy == y)
        for z in range(count_z):
            at = y * count_z + z
            for t in range(parts):
                piece = moved[:count, (z * parts + t) * 128 : (z * parts + t + 1) * 128] * own_y
                line[t * count : (t + 1) * count, :] = piece
            for c in range(3):
                to = fine_at + c * each
                source = c * 32 + at * each
                line[to : to + each, :] = buf[source : source + each, :]
            out[at] = line[...].astype(BF)


def finish(sizes, recv, fine_in, coarse_in, coarse_mid, lift, fine_out):
    count_x, count_y, count_z = sizes
    i_mid, i_fine = 128 // count_x, 32 // count_x
    _, parts = lane_tiles(sizes)
    total = recv[0].astype(F32)
    for at in range(1, count_y * count_z):
        total = total + recv[at].astype(F32)
    count = i_mid + i_fine
    wide = jnp.concatenate([total[t * count : (t + 1) * count] for t in range(parts)], axis=1)
    for o in range(128 // (count_y * count_z)):
        piece = wide[:, o * 32 : o * 32 + 27]
        for i in range(i_mid):
            coarse_mid[i, o : o + 1, :] = piece[i : i + 1]
        for i in range(i_fine):
            coarse_in[i, o : o + 1, :] = piece[i_mid + i : i_mid + i + 1]
    lift_each = 32 // (count_y * count_z)
    shape = (8, parts * 128)
    pick = ones_where(iota(shape, 1) == iota(shape, 0) * 32 + 27)
    exact = lax.Precision.HIGHEST
    moved = lax.dot_general(
        pick, wide[:i_mid], NT, preferred_element_type=F32, precision=exact
    )
    lift[...] = moved[:lift_each]
    base = parts * count
    cell = iota((8, 128), 1)
    keep = ones_where(iota((8, 128), 0) == cell // (9 * i_fine) * i_fine + cell % i_fine)
    cell = iota((384, 128), 0) % 128
    tap = cell // i_fine % 9 * 3 + iota((384, 128), 0) // 128
    tap = jnp.where(cell // (9 * i_fine) == 0, tap, 26 - tap)
    perm = ones_where((iota((384, 128), 1) == tap) & (cell < 18 * i_fine))
    for o in range(lift_each):
        rows = []
        for c in range(3):
            at = base + c * lift_each + o
            rows.append(jnp.broadcast_to(total[at : at + 1], (8, 128)) * keep)
        moved = jnp.dot(
            jnp.concatenate(rows, axis=1), perm, preferred_element_type=F32, precision=exact
        )
        for i in range(i_fine):
            fine_out[i, o : o + 1, :] = moved[i : i + 1, :27]
            fine_in[i, o : o + 1, :] = moved[i_fine + i : i_fine + i + 1, :27]


def from_below(value, axis):
    count = lax.axis_size(axis)
    return lax.ppermute(value, axis, [(i, i + 1) for i in range(count - 1)])


def from_above(value, axis):
    count = lax.axis_size(axis)
    return lax.ppermute(value, axis, [(i + 1, i) for i in range(count - 1)])


def shape_of(shape, dtype):
    return jax.ShapeDtypeStruct(shape, dtype)


def shards(features, cotangent, w_fine_in, w_coarse_in, w_coarse_mid, w_lift, w_fine_out):
    sizes = (lax.axis_size(GX), lax.axis_size(GY), lax.axis_size("gz"))
    count_x, count_y, count_z = sizes
    cells = count_x * count_y * count_z * 4 * 4 * 128
    scale = 1.0 / math.sqrt(cells)
    place = jnp.stack([lax.axis_index(GX), lax.axis_index(GY), lax.axis_index("gz")])
    place = place.astype(jnp.int32)

    own = jnp.stack([features, cotangent]).transpose(0, 2, 3, 1, 4)
    xlo = from_below(own[:, 2:4], GX)
    xhi = from_above(own[:, 0:2], GX)
    y_tail = jnp.concatenate([xlo[:, :, 2:4], own[:, :, 2:4], xhi[:, :, 2:4]], axis=1)
    y_head = jnp.concatenate([xlo[:, :, 0:2], own[:, :, 0:2], xhi[:, :, 0:2]], axis=1)
    ylo = from_below(y_tail, GY)
    yhi = from_above(y_head, GY)
    face = call(z_faces, shape_of((2, 2, 32, 128), BF), [], 5, False, 4)(own, xlo, xhi, ylo, yhi)
    face_l = from_below(face, "gz")
    face_r = from_above(face, "gz")
    taps = pltpu.VMEM((288, 96), BF)
    keep, msg = call(
        functools.partial(fine_first, sizes),
        (
            shape_of((19, 32, 768), F32),
            shape_of((32, 64), BF),
        ),
        [pltpu.VMEM((6, 32, 768), F32), pltpu.VMEM((96, 1024), BF), taps, taps],
        11,
        True,
        10,
    )(place, own, xlo, xhi, ylo, yhi, face, face_l, face_r, w_fine_in, w_fine_out)

    z_lo = from_below(msg[24:32], "gz")
    z_hi = from_above(msg[0:8], "gz")
    window = jnp.concatenate(
        [z_lo[8 - PAD :], msg, z_hi[:PAD], jnp.zeros((PITCH - OWN - 2 * PAD, 64), BF)], axis=0
    )
    packed = jnp.concatenate([window[:24], window[24:]], axis=1)
    half_y = count_y // 2
    recv = lax.all_to_all(
        jnp.broadcast_to(packed[None], (count_x * half_y, 24, 128)),
        GX + ("gy_0",),
        split_axis=0,
        concat_axis=0,
        tiled=True,
    ).reshape(count_x, half_y, 24, 128)
    recv_far = lax.ppermute(recv, "gy_1", [(0, 1), (1, 0)])

    rows = count_y * PITCH
    wide = rows + 2 * PITCH
    out, grad_input, msg = call(
        functools.partial(second, sizes, scale),
        (
            shape_of((4, 4, 32, 128), BF),
            shape_of((4, 4, 32, 128), BF),
            shape_of((count_x, message_rows(sizes), 128), BF),
        ),
        [
            pltpu.VMEM((11, rows, 64), BF),
            pltpu.VMEM((11, wide, 128), BF),
            pltpu.VMEM((9, wide, 384), BF),
            pltpu.VMEM((7, wide, 384), BF),
            pltpu.VMEM((5, wide + 2 * PITCH, 384), BF),
            pltpu.VMEM((9, rows, 128), F32),
            pltpu.VMEM((7, wide, 128), BF),
            pltpu.VMEM((384, 384), BF),
            pltpu.VMEM((1152, 384), BF),
            pltpu.VMEM((384, 1152), BF),
            pltpu.VMEM((9, 32, 384), BF),
            pltpu.VMEM((3, 3 * PITCH, 64), F32),
            pltpu.VMEM((24, 64), F32),
            pltpu.VMEM((6, 96, 768), BF),
            pltpu.VMEM((6, 96, 768), BF),
            pltpu.VMEM((4, 32, 512), F32),
            taps,
            taps,
            pltpu.VMEM((count_x, message_rows(sizes), 128), F32),
            pltpu.VMEM((27, 32, 128), BF),
            pltpu.VMEM((27, 128, 128), BF),
            pltpu.VMEM((32, 128), BF),
            pltpu.VMEM((27, 32, 32), BF),
            pltpu.VMEM((27, 32, 32), BF),
            pltpu.SemaphoreType.DMA((5,)),
        ],
        5,
        True,
        30,
        in_hbm=5,
    )(
        place, recv, recv_far, own, keep,
        w_coarse_in, w_coarse_mid, w_lift.T, w_fine_in, w_fine_out,
    )
    out = out.transpose(2, 0, 1, 3)
    grad_input = grad_input.transpose(2, 0, 1, 3)

    msg = lax.all_to_all(msg, GX, split_axis=0, concat_axis=0, tiled=True)
    msg = call(
        functools.partial(regroup, sizes),
        shape_of((count_y * count_z, final_rows(sizes), 128), BF),
        [pltpu.VMEM((128, 128), F32), pltpu.VMEM((final_rows(sizes), 128), F32)],
        3,
        True,
        6,
    )(place, msg, gz_perm(sizes))
    msg = lax.all_to_all(msg, GY + ("gz",), split_axis=0, concat_axis=0, tiled=True)
    i_mid, i_fine = 128 // count_x, 32 // count_x
    o_mid, o_fine = 128 // (count_y * count_z), 32 // (count_y * count_z)
    grads = call(
        functools.partial(finish, sizes),
        (
            shape_of((i_fine, o_fine, 27), F32),
            shape_of((i_fine, o_mid, 27), F32),
            shape_of((i_mid, o_mid, 27), F32),
            shape_of((o_fine, i_mid), F32),
            shape_of((i_fine, o_fine, 27), F32),
        ),
        [],
        1,
        False,
        6,
        False,
    )(msg)
    fine_in, coarse_in, coarse_mid, lift, fine_out = grads
    return (
        out,
        grad_input,
        fine_in.transpose(2, 0, 1),
        coarse_in.transpose(2, 0, 1),
        coarse_mid.transpose(2, 0, 1),
        lift.T,
        fine_out.transpose(2, 0, 1),
    )


def solution(mesh):
    shape = mesh.shape
    split = Mesh(
        mesh.devices.reshape(shape["gx"] // 2, 2, shape["gy"] // 2, 2, shape["gz"]),
        GX + GY + ("gz",),
    )
    field = P(None, GX, GY, "gz")
    grad = P(None, GX, GY + ("gz",))
    return jax.shard_map(
        shards,
        mesh=split,
        in_specs=(field, field, P(), P(), P(), P(), P()),
        out_specs=(field, field, grad, grad, grad, P(GX, GY + ("gz",)), grad),
        check_vma=False,
    )
```

```python
import functools
import math

import jax
import jax.numpy as jnp
import numpy as np
from jax import lax
from jax.experimental import pallas as pl
from jax.experimental.pallas import tpu as pltpu
from jax.sharding import Mesh
from jax.sharding import PartitionSpec as P

GX = ("gx_0", "gx_1")
GY = ("gy_0", "gy_1")
INTERPRET = False
BF = jnp.bfloat16
F32 = jnp.float32
PAD = 5
OWN = 32
PITCH = 48
NT = (((1,), (1,)), ((), ()))
TN = (((0,), (0,)), ((), ()))
COARSE_OF = (0, 1, 1, 1, 1, 2)


def mm(lhs, rhs):
    return jnp.dot(lhs, rhs, preferred_element_type=F32)


def mm_nt(lhs, rhs):
    return lax.dot_general(lhs, rhs, NT, preferred_element_type=F32)


def mm_tn(lhs, rhs):
    return lax.dot_general(lhs, rhs, TN, preferred_element_type=F32)


def lane_roll(value, shift):
    return pltpu.roll(value, shift % value.shape[1], 1)


def row_roll(value, shift):
    return pltpu.roll(value, shift % value.shape[0], 0)


def call(body, out_shape, scratch, n_in, smem_first, megabytes, keep_out=True, in_hbm=0):
    spec = [pl.BlockSpec(memory_space=pltpu.VMEM)] * n_in
    if smem_first:
        spec[0] = pl.BlockSpec(memory_space=pltpu.SMEM)
    spec = spec + [pl.BlockSpec(memory_space=pl.ANY)] * in_hbm
    out_spec = pl.BlockSpec(memory_space=pltpu.VMEM) if keep_out else pl.BlockSpec()
    return pl.pallas_call(
        body,
        out_shape=out_shape,
        in_specs=spec,
        out_specs=jax.tree.map(lambda _: out_spec, out_shape),
        scratch_shapes=scratch,
        compiler_params=pltpu.CompilerParams(vmem_limit_bytes=megabytes * 1024 * 1024),
        interpret=INTERPRET,
    )


def rows_of(own, xlo, xhi, ylo, yhi):
    def row(arr, xi, yi):
        if yi < 2:
            return ylo[arr, xi, yi]
        if yi >= 6:
            return yhi[arr, xi, yi - 6]
        if xi < 2:
            return xlo[arr, xi, yi - 2]
        if xi >= 6:
            return xhi[arr, xi - 6, yi - 2]
        return own[arr, xi - 2, yi - 2]

    return row


def iota(shape, dim):
    return lax.broadcasted_iota(jnp.int32, shape, dim)


def ones_where(flag):
    return jnp.where(flag, 1.0, 0.0)


def z_faces(own, xlo, xhi, ylo, yhi, out):
    row = rows_of(own, xlo, xhi, ylo, yhi)
    lane = iota((32, 128), 1)
    column = iota((256, 256), 1)
    source = jnp.where(column < 128, 0, 1)
    source = jnp.where(column % 128 < 64, source, 3 - source)
    perm = ones_where(iota((256, 256), 0) == column % 64 * 4 + source).astype(BF)
    for arr in range(2):
        halves = []
        for half in range(2):
            gathered = jnp.zeros((32, 128), F32)
            for at in range(32):
                cell = half * 32 + at
                value = row(arr, cell // 8, cell % 8).astype(F32)
                moved = lane_roll(value, 4 * at + 2)
                here = (lane >= 4 * at) & (lane < 4 * at + 4)
                gathered = jnp.where(here, moved, gathered)
            halves.append(gathered.astype(BF))
        tiles = mm(jnp.concatenate(halves, axis=1), perm).astype(BF)
        out[arr, 0] = tiles[:, :128]
        out[arr, 1] = tiles[:, 128:]


def stacked_row(value, edge, cell, lane):
    before = jnp.where(lane == 0, lane_roll(edge, -cell), lane_roll(value, 1))
    after = jnp.where(lane == 127, lane_roll(edge, 63 - cell), lane_roll(value, -1))
    return jnp.concatenate([before, value, after], axis=0).astype(BF)


def edge_sum(weight, tile):
    product = mm(weight, tile)
    total = None
    for ab in range(9):
        part = lane_roll(product[ab * 32 : ab * 32 + 32], -(ab // 3 * 8 + ab % 3))
        total = part if total is None else total + part
    return total


def slope_of(value):
    sigma = jax.nn.sigmoid(value)
    return sigma, sigma * (1.0 + value * (1.0 - sigma))


def forward_taps(weight, store):
    same = ones_where(iota((32, 32), 0) == iota((32, 32), 1)).astype(BF)
    for ab in range(9):
        stack = jnp.concatenate([weight[3 * ab + c] for c in range(3)], axis=0)
        store[ab * 32 : ab * 32 + 32, :] = mm_nt(same, stack).astype(BF)


def backward_taps(weight, store):
    for ab in range(9):
        stack = [weight[26 - 3 * ab - c].astype(F32) for c in range(3)]
        store[ab * 32 : ab * 32 + 32, :] = jnp.concatenate(stack, axis=1).astype(BF)


def fine_first(
    sizes, place, own, xlo, xhi, ylo, yhi, face, face_l, face_r, w_fine_in, w_fine_out,
    keep, msg, acc, vbuf, w_z, w_d,
):
    count_x, count_y, count_z = sizes
    gx, gy, gz = place[0], place[1], place[2]
    row = rows_of(own, xlo, xhi, ylo, yhi)
    lane = iota((32, 128), 1)
    lower = lane < 64
    x_in = [gx > 0, None, None, None, None, gx < count_x - 1]
    y_in = [gy > 0, None, None, None, None, gy < count_y - 1]
    forward_taps(w_fine_in, w_z)
    backward_taps(w_fine_out, w_d)

    def factor(flag):
        return 1.0 if flag is None else jnp.where(flag, 1.0, 0.0)

    pooled = {}
    pool = ones_where(iota((32, 128), 1) // 4 == iota((32, 128), 0))
    for arr, weight in ((0, w_z), (1, w_d)):
        tile_a, tile_b = face[arr, 0].astype(F32), face[arr, 1].astype(F32)
        left_a, left_b = face_l[arr, 0].astype(F32), face_l[arr, 1].astype(F32)
        right_a, right_b = face_r[arr, 0].astype(F32), face_r[arr, 1].astype(F32)
        swapped = lane_roll(tile_b, 64)
        edge_0 = jnp.where(lower, left_a, swapped)
        edge_1 = jnp.where(lower, left_b, right_b)
        edge_2 = jnp.where(lower, swapped, right_a)
        edges = edge_sum(weight[...], jnp.concatenate([edge_0, edge_1, edge_2], axis=0).astype(BF))
        def stack_plane(xi):
            for yi in range(8):
                value = row(arr, xi, yi).astype(F32)
                line = stacked_row(value, edge_1, xi * 8 + yi, lane)
                vbuf[xi % 2, :, yi * 128 : yi * 128 + 128] = line

        stack_plane(0)
        for xi in range(8):
            if xi < 7:
                stack_plane(xi + 1)
            product = mm(weight[...], vbuf[xi % 2])
            for a in range(3):
                m = xi - a
                if 0 <= m < 6:
                    part = None
                    for b in range(3):
                        at = (3 * a + b) * 32
                        piece = product[at : at + 32, b * 128 : b * 128 + 768]
                        part = piece if part is None else part + piece
                    acc[m] = part if a == 0 else acc[m] + part
        total = jnp.zeros((32, 128), F32)
        if arr == 0:
            x_at = lane % 64 // 8
            y_at = lane % 8
            inside = jnp.where(lower, factor(gz > 0), factor(gz < count_z - 1))
            inside = inside * jnp.where(x_at == 0, factor(x_in[0]), 1.0)
            inside = inside * jnp.where(x_at == 5, factor(x_in[5]), 1.0)
            inside = inside * jnp.where(y_at == 0, factor(y_in[0]), 1.0)
            inside = inside * jnp.where(y_at == 5, factor(y_in[5]), 1.0)
            sigma, steep = slope_of(edges)
            keep[18, :, 0:128] = (edges * sigma * inside).astype(BF).astype(F32)
            keep[18, :, 128:256] = steep * inside
            for m in range(6):
                for k in range(6):
                    at = slice(k * 128, k * 128 + 128)
                    mask = factor(x_in[m]) * factor(y_in[k])
                    value = acc[m, :, at]
                    sigma, steep = slope_of(value)
                    first = (value * sigma * mask).astype(BF)
                    keep[m, :, at] = first.astype(F32)
                    keep[6 + m, :, at] = steep * mask
                    if 1 <= m < 5 and 1 <= k < 5:
                        total = total + first.astype(F32)
            total = total * (1.0 / 64.0)
        else:
            keep[18, :, 256:384] = edges
            for m in range(6):
                keep[12 + m] = acc[m]
                if 1 <= m < 5:
                    for k in range(1, 5):
                        total = total + acc[m, :, k * 128 : k * 128 + 128]
        pooled[arr] = lax.dot_general(
            pool, total, NT, preferred_element_type=F32, precision=lax.Precision.HIGHEST
        )
    msg[...] = jnp.concatenate([pooled[0], pooled[1]], axis=1).astype(BF)


def split_two(value):
    high = value.astype(BF)
    low = (value - high.astype(F32)).astype(BF)
    return jnp.concatenate([high, low], axis=0)


def lane_tiles(sizes):
    count_x, count_y, count_z = sizes
    span, lift = 128 // count_y, 32 // count_y
    first = -(-(27 * span + lift) // 128)
    second = -(-(span // count_z * 32) // 128)
    return first, second


def message_rows(sizes):
    i_mid, i_fine = 128 // sizes[0], 32 // sizes[0]
    tiles, _ = lane_tiles(sizes)
    used = tiles * i_mid + tiles * i_fine + 18 * i_fine
    return -(-used // 16) * 16


def final_rows(sizes):
    i_mid, i_fine = 128 // sizes[0], 32 // sizes[0]
    _, tiles = lane_tiles(sizes)
    used = tiles * i_mid + tiles * i_fine + 3 * (32 // (sizes[1] * sizes[2]))
    return -(-used // 16) * 16


def second(
    sizes, scale, place, recv, recv_far, own, keep,
    w_in_hbm, w_mid_hbm, w_lift_hbm, w_fine_in_hbm, w_fine_out_hbm,
    out, g_in, msg,
    raw, p3, c3, d3, e3, s2, c2, wp_in, wp_mid, bp_mid, b_in, lds, edge_rows,
    v_join, v_dz, acc, w_o, w_g, mbuf, w_in, w_mid, w_lift, w_fine_in, w_fine_out, arrived,
):
    count_x, count_y, count_z = sizes
    loads = [
        pltpu.make_async_copy(source, target, arrived.at[at])
        for at, (source, target) in enumerate(
            (
                (w_in_hbm, w_in),
                (w_mid_hbm, w_mid),
                (w_lift_hbm, w_lift),
                (w_fine_in_hbm, w_fine_in),
                (w_fine_out_hbm, w_fine_out),
            )
        )
    ]
    for load in loads:
        load.start()
    gx, gy, gz = place[0], place[1], place[2]
    rows = count_y * PITCH
    body_rows = slice(PITCH, PITCH + rows)
    deep_rows = slice(2 * PITCH, 2 * PITCH + rows)

    z_at = iota((PITCH, 128), 0)
    z_all = z_at + (gz * OWN - PAD)
    z_mask = ones_where((z_all >= 0) & (z_all < count_z * OWN))
    z_mask = jnp.concatenate([z_mask] * count_y, axis=0)
    own_mask = ones_where((z_at >= PAD) & (z_at < PAD + OWN))
    own_mask = jnp.concatenate([own_mask] * count_y, axis=0)

    for store, pads in ((p3, 1), (c3, 1), (d3, 1), (e3, 2), (c2, 1)):
        for plane in range(store.shape[0]):
            blank = jnp.zeros((pads * PITCH, store.shape[2]), BF)
            store[plane, 0 : pads * PITCH] = blank
            store[plane, pads * PITCH + rows : 2 * pads * PITCH + rows] = blank
    def inside(plane):
        at = gx + plane - PAD
        return (at >= 0) & (at < count_x), jnp.clip(at, 0, count_x - 1)

    def stacked(value):
        return jnp.concatenate([row_roll(value, 1), value, row_roll(value, -1)], axis=1).astype(BF)

    def unpack(plane):
        ok, at = inside(plane)
        valid = ones_where(ok)
        parts = []
        for y in range(count_y):
            near_by = lax.rem(gy, 2) == y % 2
            block = jnp.where(near_by, recv[at, y // 2], recv_far[at, y // 2]).astype(F32) * valid
            parts.append(block[:, :64])
            parts.append(block[:, 64:])
        whole = jnp.concatenate(parts, axis=0)
        raw[plane] = whole.astype(BF)
        first = whole[:, :32]
        around = [row_roll(first, 1), first, row_roll(first, -1), jnp.zeros((rows, 32), F32)]
        p3[plane, body_rows, :] = jnp.concatenate(around, axis=1).astype(BF)

    for load in loads:
        load.wait()
    wp_in[...] = jnp.zeros(wp_in.shape, BF)
    for a in range(3):
        for b in range(3):
            for c in range(3):
                tap = 9 * a + 3 * b + c
                side = slice(b * 128, b * 128 + 128)
                deep = slice(a * 384 + c * 128, a * 384 + c * 128 + 128)
                wp_in[a * 128 + c * 32 : a * 128 + c * 32 + 32, side] = w_in[tap]
                wp_mid[deep, side] = w_mid[tap]
                bp_mid[side, deep] = w_mid[26 - tap]
                b_in[3 * a + b, :, c * 128 : c * 128 + 128] = w_in[26 - tap]

    def taps(store, first, pair, alone, product):
        top = [store[first + a, 0 : rows + PITCH, :] for a in range(3)]
        end = [store[first + a, 2 * PITCH : 2 * PITCH + rows, :] for a in range(3)]
        both = product(jnp.concatenate(top, axis=1), pair)
        last = product(jnp.concatenate(end, axis=1), alone)
        return both[:rows, :128] + both[PITCH:, 128:] + last

    def level_2(plane):
        ok, _ = inside(plane)
        mask = z_mask * ones_where(ok)
        z_2 = taps(p3, plane - 1, wp_in[:, :256], wp_in[:, 256:], mm)
        sigma, steep = slope_of(z_2)
        s2[plane - 1] = steep * mask
        c3[plane - 1, body_rows, :] = stacked(z_2 * sigma * mask)

    lift_64 = jnp.concatenate([jnp.zeros((32, 128), BF), w_lift[...]], axis=0)

    def level_3(plane):
        ok, _ = inside(plane)
        mask = z_mask * ones_where(ok)
        z_3 = taps(c3, plane - 2, wp_mid[:, :256], wp_mid[:, 256:], mm)
        sigma, steep = slope_of(z_3)
        c2[plane - 2, body_rows, :] = (z_3 * sigma * mask).astype(BF)
        d_third = mm(raw[plane], lift_64)
        d3[plane - 2, body_rows, :] = stacked(d_third * steep)

    def level_2_back(plane):
        total = taps(d3, plane - 3, bp_mid[:256, :], bp_mid[256:, :], mm_nt)
        e3[plane - 3, deep_rows, :] = stacked(total * s2[plane - 1])

    for step in range(14):
        if step < 11:
            unpack(step)
        if 1 <= step - 1 < 10:
            level_2(step - 1)
        if 2 <= step - 2 < 9:
            level_3(step - 2)
        if 3 <= step - 3 < 8:
            level_2_back(step - 3)

    near = 3 * PITCH
    for x in range(3):
        d_pool = None
        for ab in range(9):
            start = pl.multiple_of((gy + ab % 3) * PITCH, PITCH)
            part = mm_nt(e3[x + ab // 3, pl.ds(start, near), :], b_in[ab])
            d_pool = part if d_pool is None else d_pool + part
        lifted = mm_nt(c2[2 + x, pl.ds(pl.multiple_of(gy * PITCH, PITCH), near), :], w_lift[...])
        lds[x] = jnp.concatenate([lifted, d_pool], axis=1)

    span, lift_span = 128 // count_y, 32 // count_y
    tiles, _ = lane_tiles(sizes)
    lanes = tiles * 128
    col = iota((384, 3 * span), 1)
    share = iota((384, 3 * span), 0) == col // span * 128 + col % span + gy * span
    share = ones_where(share).astype(BF)

    def shifted(store, first, pads):
        parts = []
        for a in range(3):
            picked = mm(store[first + a], share)
            for b in range(3):
                start = (pads - 1 + b) * PITCH
                parts.append(picked[start : start + rows])
        parts.append(jnp.zeros((rows, lanes - 27 * span), F32))
        return jnp.concatenate(parts, axis=1).astype(BF)

    c1_own = (c3[4, body_rows, 128:256].astype(F32) * own_mask).astype(BF)
    c2_own = (c2[3, body_rows, :].astype(F32) * own_mask).astype(BF)
    raw_own = (raw[5].astype(F32) * own_mask[:, :64]).astype(BF)
    col = iota((64, lanes), 1) - 27 * span
    pick = (iota((64, lanes), 0) == col + 32 + gy * lift_span) & (col >= 0) & (col < lift_span)
    d_lift = mm(raw[5], ones_where(pick).astype(BF)).astype(BF)
    g_mid = (mm_tn(c1_own, shifted(d3, 2, 1)) + mm_tn(c2_own, d_lift)) * scale
    g_coarse = mm_tn(raw_own, shifted(e3, 1, 2)) * scale
    i_mid, i_fine = 128 // count_x, 32 // count_x
    for x in range(count_x):
        for tile in range(tiles):
            at = slice(tile * 128, tile * 128 + 128)
            to = tile * i_mid
            mbuf[x, to : to + i_mid, :] = g_mid[x * i_mid : (x + 1) * i_mid, at]
            to = tiles * i_mid + tile * i_fine
            mbuf[x, to : to + i_fine, :] = g_coarse[x * i_fine : (x + 1) * i_fine, at]

    forward_taps(w_fine_out, w_o)
    backward_taps(w_fine_in, w_g)
    lane = iota((32, 128), 1)
    up = ones_where(iota((PITCH, 128), 0) == iota((PITCH, 128), 1) // 4 + PAD).astype(BF)
    up = jnp.concatenate([up, up], axis=0)
    spread = {}
    for x in range(3):
        for y in range(3):
            spread[x, y] = mm_tn(split_two(lds[x, y * PITCH : y * PITCH + PITCH]), up)
    edge_rows[...] = jnp.zeros(edge_rows.shape, F32)
    for side in range(2):
        for x in range(3):
            for y in range(3):
                at = side * 9 + x * 3 + y
                z = y * PITCH + (PAD - 1 if side == 0 else PAD + OWN)
                edge_rows[at : at + 1, :] = lds[x, z : z + 1, :]
    cell = iota((24, 128), 1)
    x_at, y_at = cell % 64 // 8, cell % 8
    x_of = jnp.where(x_at == 0, 0, jnp.where(x_at == 5, 2, 1))
    y_of = jnp.where(y_at == 0, 0, jnp.where(y_at == 5, 2, 1))
    edge_up = iota((24, 128), 0) == cell // 64 * 9 + x_of * 3 + y_of
    edge_up = ones_where(edge_up & (x_at < 6) & (y_at < 6))
    edge_up = jnp.concatenate([edge_up, edge_up], axis=0).astype(BF)
    spread_e = mm_tn(split_two(edge_rows[...]), edge_up)
    join_e = (keep[18, :, 0:128] + spread_e[:32]).astype(BF).astype(F32)
    dz_e = (keep[18, :, 256:384] + spread_e[32:] * (1.0 / 64.0)) * keep[18, :, 128:256]
    dz_e = dz_e.astype(BF).astype(F32)
    def stack_plane(m):
        for k in range(6):
            at = slice(k * 128, k * 128 + 128)
            over = spread[COARSE_OF[m], COARSE_OF[k]]
            join = (keep[m, :, at] + over[:32]).astype(BF).astype(F32)
            v_join[m, :, at] = stacked_row(join, join_e, m * 8 + k, lane)
            dz = (keep[12 + m, :, at] + over[32:] * (1.0 / 64.0)) * keep[6 + m, :, at]
            v_dz[m, :, at] = stacked_row(dz.astype(BF).astype(F32), dz_e, m * 8 + k, lane)

    stack_plane(0)
    for m in range(6):
        if m < 5:
            stack_plane(m + 1)
        for kind, (store, weight) in enumerate(((v_join, w_o), (v_dz, w_g))):
            product = mm(weight[...], store[m])
            for a in range(3):
                x = m - a
                if 0 <= x < 4:
                    part = None
                    for b in range(3):
                        at = (3 * a + b) * 32
                        piece = product[at : at + 32, b * 128 : b * 128 + 512]
                        part = piece if part is None else part + piece
                    if a == 0:
                        acc[kind, x] = part
                    elif a == 1:
                        acc[kind, x] = acc[kind, x] + part
                    else:
                        part = (acc[kind, x] + part).astype(BF)
                        for y in range(4):
                            (out, g_in)[kind][x, y] = part[:, y * 128 : y * 128 + 128]
    flat = [
        [jnp.concatenate([own[arr, x, y] for y in range(4)], axis=1) for x in range(4)]
        for arr in range(2)
    ]
    base = tiles * (i_mid + i_fine)
    for ab in range(9):
        a, b = ab // 3, ab % 3
        at = slice(b * 128, b * 128 + 512)
        total_o = None
        total_i = None
        for x in range(4):
            part_o = mm_nt(v_join[x + a, :, at], flat[1][x])
            part_i = mm_nt(flat[0][x], v_dz[x + a, :, at])
            total_o = part_o if total_o is None else total_o + part_o
            total_i = part_i if total_i is None else total_i + part_i
        by_tap = [total_o[c * 32 : c * 32 + 32] for c in range(3)]
        blank = jnp.zeros((32, 32), F32)
        total_o = jnp.concatenate([*by_tap, blank], axis=1)
        both = (total_o * scale, jnp.concatenate([total_i, blank], axis=1) * scale)
        for kind in range(2):
            to = base + (kind * 9 + ab) * i_fine
            for x in range(count_x):
                mbuf[x, to : to + i_fine, :] = both[kind][x * i_fine : (x + 1) * i_fine]
    used = base + 18 * i_fine
    for x in range(count_x):
        if used < mbuf.shape[1]:
            mbuf[x, used:, :] = jnp.zeros((mbuf.shape[1] - used, 128), F32)
        msg[x] = mbuf[x].astype(BF)


def gz_perm(sizes):
    count_x, count_y, count_z = sizes
    tiles, parts = lane_tiles(sizes)
    span, lift = 128 // count_y, 32 // count_y
    each, lift_each = span // count_z, lift // count_z
    perm = np.zeros((tiles * 128, count_z * parts * 128), np.float32)
    for z in range(count_z):
        base = z * parts * 128
        for tap in range(27):
            for o in range(each):
                perm[tap * span + z * each + o, base + o * 32 + 26 - tap] = 1
        for o in range(lift_each):
            perm[27 * span + z * lift_each + o, base + o * 32 + 27] = 1
    return jnp.asarray(perm, BF)


def split_three(value):
    high = value.astype(BF)
    rest = value - high.astype(F32)
    mid = rest.astype(BF)
    low = (rest - mid.astype(F32)).astype(BF)
    return high, mid, low


def regroup(sizes, place, recv, perm, out, buf, line):
    count_x, count_y, count_z = sizes
    gy = place[1]
    i_mid, i_fine = 128 // count_x, 32 // count_x
    tiles, parts = lane_tiles(sizes)
    total = recv[0].astype(F32)
    for x in range(1, count_x):
        total = total + recv[x].astype(F32)
    base = tiles * i_mid
    mid = jnp.concatenate([total[t * i_mid : (t + 1) * i_mid] for t in range(tiles)], axis=1)
    low = [total[base + t * i_fine : base + (t + 1) * i_fine] for t in range(tiles)]
    low = jnp.concatenate(low, axis=1)
    count = i_mid + i_fine
    padded = -(-count // 16) * 16
    blank = jnp.zeros((padded - count, tiles * 128), F32)
    coarse = jnp.concatenate([mid, low, blank], axis=0)
    moved = None
    for part in split_three(coarse):
        term = mm(part, perm[...])
        moved = term if moved is None else moved + term
    base = tiles * (i_mid + i_fine)
    fine = total[base : base + 18 * i_fine]
    fine = jnp.concatenate([fine, jnp.zeros((128 - 18 * i_fine, 128), F32)], axis=0)
    buf[...] = jnp.transpose(fine)
    each = 32 // (count_y * count_z)
    fine_at = parts * count
    line[...] = jnp.zeros(line.shape, F32)
    for y in range(count_y):
        own_y = ones_where(gy == y)
        for z in range(count_z):
            at = y * count_z + z
            for t in range(parts):
                piece = moved[:count, (z * parts + t) * 128 : (z * parts + t + 1) * 128] * own_y
                line[t * count : (t + 1) * count, :] = piece
            for c in range(3):
                to = fine_at + c * each
                source = c * 32 + at * each
                line[to : to + each, :] = buf[source : source + each, :]
            out[at] = line[...].astype(BF)


def finish(sizes, recv, fine_in, coarse_in, coarse_mid, lift, fine_out):
    count_x, count_y, count_z = sizes
    i_mid, i_fine = 128 // count_x, 32 // count_x
    _, parts = lane_tiles(sizes)
    total = recv[0].astype(F32)
    for at in range(1, count_y * count_z):
        total = total + recv[at].astype(F32)
    count = i_mid + i_fine
    wide = jnp.concatenate([total[t * count : (t + 1) * count] for t in range(parts)], axis=1)
    for o in range(128 // (count_y * count_z)):
        piece = wide[:, o * 32 : o * 32 + 27]
        for i in range(i_mid):
            coarse_mid[i, o : o + 1, :] = piece[i : i + 1]
        for i in range(i_fine):
            coarse_in[i, o : o + 1, :] = piece[i_mid + i : i_mid + i + 1]
    lift_each = 32 // (count_y * count_z)
    shape = (8, parts * 128)
    pick = ones_where(iota(shape, 1) == iota(shape, 0) * 32 + 27)
    exact = lax.Precision.HIGHEST
    moved = lax.dot_general(
        pick, wide[:i_mid], NT, preferred_element_type=F32, precision=exact
    )
    lift[...] = moved[:lift_each]
    base = parts * count
    cell = iota((8, 128), 1)
    keep = ones_where(iota((8, 128), 0) == cell // (9 * i_fine) * i_fine + cell % i_fine)
    cell = iota((384, 128), 0) % 128
    tap = cell // i_fine % 9 * 3 + iota((384, 128), 0) // 128
    tap = jnp.where(cell // (9 * i_fine) == 0, tap, 26 - tap)
    perm = ones_where((iota((384, 128), 1) == tap) & (cell < 18 * i_fine))
    for o in range(lift_each):
        rows = []
        for c in range(3):
            at = base + c * lift_each + o
            rows.append(jnp.broadcast_to(total[at : at + 1], (8, 128)) * keep)
        moved = jnp.dot(
            jnp.concatenate(rows, axis=1), perm, preferred_element_type=F32, precision=exact
        )
        for i in range(i_fine):
            fine_out[i, o : o + 1, :] = moved[i : i + 1, :27]
            fine_in[i, o : o + 1, :] = moved[i_fine + i : i_fine + i + 1, :27]


def from_below(value, axis):
    count = lax.axis_size(axis)
    return lax.ppermute(value, axis, [(i, i + 1) for i in range(count - 1)])


def from_above(value, axis):
    count = lax.axis_size(axis)
    return lax.ppermute(value, axis, [(i + 1, i) for i in range(count - 1)])


def shape_of(shape, dtype):
    return jax.ShapeDtypeStruct(shape, dtype)


def shards(features, cotangent, w_fine_in, w_coarse_in, w_coarse_mid, w_lift, w_fine_out):
    sizes = (lax.axis_size(GX), lax.axis_size(GY), lax.axis_size("gz"))
    count_x, count_y, count_z = sizes
    cells = count_x * count_y * count_z * 4 * 4 * 128
    scale = 1.0 / math.sqrt(cells)
    place = jnp.stack([lax.axis_index(GX), lax.axis_index(GY), lax.axis_index("gz")])
    place = place.astype(jnp.int32)

    own = jnp.stack([features, cotangent]).transpose(0, 2, 3, 1, 4)
    xlo = from_below(own[:, 2:4], GX)
    xhi = from_above(own[:, 0:2], GX)
    y_tail = jnp.concatenate([xlo[:, :, 2:4], own[:, :, 2:4], xhi[:, :, 2:4]], axis=1)
    y_head = jnp.concatenate([xlo[:, :, 0:2], own[:, :, 0:2], xhi[:, :, 0:2]], axis=1)
    ylo = from_below(y_tail, GY)
    yhi = from_above(y_head, GY)
    face = call(z_faces, shape_of((2, 2, 32, 128), BF), [], 5, False, 4)(own, xlo, xhi, ylo, yhi)
    face_l = from_below(face, "gz")
    face_r = from_above(face, "gz")
    taps = pltpu.VMEM((288, 96), BF)
    keep, msg = call(
        functools.partial(fine_first, sizes),
        (
            shape_of((19, 32, 768), F32),
            shape_of((32, 64), BF),
        ),
        [pltpu.VMEM((6, 32, 768), F32), pltpu.VMEM((2, 96, 1024), BF), taps, taps],
        11,
        True,
        10,
    )(place, own, xlo, xhi, ylo, yhi, face, face_l, face_r, w_fine_in, w_fine_out)

    z_lo = from_below(msg[24:32], "gz")
    z_hi = from_above(msg[0:8], "gz")
    window = jnp.concatenate(
        [z_lo[8 - PAD :], msg, z_hi[:PAD], jnp.zeros((PITCH - OWN - 2 * PAD, 64), BF)], axis=0
    )
    packed = jnp.concatenate([window[:24], window[24:]], axis=1)
    half_y = count_y // 2
    recv = lax.all_to_all(
        jnp.broadcast_to(packed[None], (count_x * half_y, 24, 128)),
        GX + ("gy_0",),
        split_axis=0,
        concat_axis=0,
        tiled=True,
    ).reshape(count_x, half_y, 24, 128)
    recv_far = lax.ppermute(recv, "gy_1", [(0, 1), (1, 0)])

    rows = count_y * PITCH
    wide = rows + 2 * PITCH
    out, grad_input, msg = call(
        functools.partial(second, sizes, scale),
        (
            shape_of((4, 4, 32, 128), BF),
            shape_of((4, 4, 32, 128), BF),
            shape_of((count_x, message_rows(sizes), 128), BF),
        ),
        [
            pltpu.VMEM((11, rows, 64), BF),
            pltpu.VMEM((11, wide, 128), BF),
            pltpu.VMEM((9, wide, 384), BF),
            pltpu.VMEM((7, wide, 384), BF),
            pltpu.VMEM((5, wide + 2 * PITCH, 384), BF),
            pltpu.VMEM((9, rows, 128), F32),
            pltpu.VMEM((7, wide, 128), BF),
            pltpu.VMEM((384, 384), BF),
            pltpu.VMEM((1152, 384), BF),
            pltpu.VMEM((384, 1152), BF),
            pltpu.VMEM((9, 32, 384), BF),
            pltpu.VMEM((3, 3 * PITCH, 64), F32),
            pltpu.VMEM((24, 64), F32),
            pltpu.VMEM((6, 96, 768), BF),
            pltpu.VMEM((6, 96, 768), BF),
            pltpu.VMEM((2, 4, 32, 512), F32),
            taps,
            taps,
            pltpu.VMEM((count_x, message_rows(sizes), 128), F32),
            pltpu.VMEM((27, 32, 128), BF),
            pltpu.VMEM((27, 128, 128), BF),
            pltpu.VMEM((32, 128), BF),
            pltpu.VMEM((27, 32, 32), BF),
            pltpu.VMEM((27, 32, 32), BF),
            pltpu.SemaphoreType.DMA((5,)),
        ],
        5,
        True,
        30,
        in_hbm=5,
    )(
        place, recv, recv_far, own, keep,
        w_coarse_in, w_coarse_mid, w_lift.T, w_fine_in, w_fine_out,
    )
    out = out.transpose(2, 0, 1, 3)
    grad_input = grad_input.transpose(2, 0, 1, 3)

    msg = lax.all_to_all(msg, GX, split_axis=0, concat_axis=0, tiled=True)
    msg = call(
        functools.partial(regroup, sizes),
        shape_of((count_y * count_z, final_rows(sizes), 128), BF),
        [pltpu.VMEM((128, 128), F32), pltpu.VMEM((final_rows(sizes), 128), F32)],
        3,
        True,
        6,
    )(place, msg, gz_perm(sizes))
    msg = lax.all_to_all(msg, GY + ("gz",), split_axis=0, concat_axis=0, tiled=True)
    i_mid, i_fine = 128 // count_x, 32 // count_x
    o_mid, o_fine = 128 // (count_y * count_z), 32 // (count_y * count_z)
    grads = call(
        functools.partial(finish, sizes),
        (
            shape_of((i_fine, o_fine, 27), F32),
            shape_of((i_fine, o_mid, 27), F32),
            shape_of((i_mid, o_mid, 27), F32),
            shape_of((o_fine, i_mid), F32),
            shape_of((i_fine, o_fine, 27), F32),
        ),
        [],
        1,
        False,
        6,
        False,
    )(msg)
    fine_in, coarse_in, coarse_mid, lift, fine_out = grads
    return (
        out,
        grad_input,
        fine_in.transpose(2, 0, 1),
        coarse_in.transpose(2, 0, 1),
        coarse_mid.transpose(2, 0, 1),
        lift.T,
        fine_out.transpose(2, 0, 1),
    )


def solution(mesh):
    shape = mesh.shape
    split = Mesh(
        mesh.devices.reshape(shape["gx"] // 2, 2, shape["gy"] // 2, 2, shape["gz"]),
        GX + GY + ("gz",),
    )
    field = P(None, GX, GY, "gz")
    grad = P(None, GX, GY + ("gz",))
    return jax.shard_map(
        shards,
        mesh=split,
        in_specs=(field, field, P(), P(), P(), P(), P()),
        out_specs=(field, field, grad, grad, grad, P(GX, GY + ("gz",)), grad),
        check_vma=False,
    )
```

```python
import functools
import math

import jax
import jax.numpy as jnp
import numpy as np
from jax import lax
from jax.experimental import pallas as pl
from jax.experimental.pallas import tpu as pltpu
from jax.sharding import Mesh
from jax.sharding import PartitionSpec as P

GX = ("gx_0", "gx_1")
GY = ("gy_0", "gy_1")
INTERPRET = False
BF = jnp.bfloat16
F32 = jnp.float32
PAD = 5
OWN = 32
PITCH = 48
NT = (((1,), (1,)), ((), ()))
TN = (((0,), (0,)), ((), ()))
COARSE_OF = (0, 1, 1, 1, 1, 2)


def mm(lhs, rhs):
    return jnp.dot(lhs, rhs, preferred_element_type=F32)


def mm_nt(lhs, rhs):
    return lax.dot_general(lhs, rhs, NT, preferred_element_type=F32)


def mm_tn(lhs, rhs):
    return lax.dot_general(lhs, rhs, TN, preferred_element_type=F32)


def lane_roll(value, shift):
    return pltpu.roll(value, shift % value.shape[1], 1)


def row_roll(value, shift):
    return pltpu.roll(value, shift % value.shape[0], 0)


def call(body, out_shape, scratch, n_in, smem_first, megabytes, keep_out=True, in_hbm=0):
    spec = [pl.BlockSpec(memory_space=pltpu.VMEM)] * n_in
    if smem_first:
        spec[0] = pl.BlockSpec(memory_space=pltpu.SMEM)
    spec = spec + [pl.BlockSpec(memory_space=pl.ANY)] * in_hbm
    out_spec = pl.BlockSpec(memory_space=pltpu.VMEM) if keep_out else pl.BlockSpec()
    return pl.pallas_call(
        body,
        out_shape=out_shape,
        in_specs=spec,
        out_specs=jax.tree.map(lambda _: out_spec, out_shape),
        scratch_shapes=scratch,
        compiler_params=pltpu.CompilerParams(vmem_limit_bytes=megabytes * 1024 * 1024),
        interpret=INTERPRET,
    )


def rows_of(own, xlo, xhi, ylo, yhi):
    def row(arr, xi, yi):
        if yi < 2:
            return ylo[arr, xi, yi]
        if yi >= 6:
            return yhi[arr, xi, yi - 6]
        if xi < 2:
            return xlo[arr, xi, yi - 2]
        if xi >= 6:
            return xhi[arr, xi - 6, yi - 2]
        return own[arr, xi - 2, yi - 2]

    return row


def iota(shape, dim):
    return lax.broadcasted_iota(jnp.int32, shape, dim)


def ones_where(flag):
    return jnp.where(flag, 1.0, 0.0)


def z_faces(own, xlo, xhi, ylo, yhi, out):
    row = rows_of(own, xlo, xhi, ylo, yhi)
    lane = iota((32, 128), 1)
    column = iota((256, 256), 1)
    source = jnp.where(column < 128, 0, 1)
    source = jnp.where(column % 128 < 64, source, 3 - source)
    perm = ones_where(iota((256, 256), 0) == column % 64 * 4 + source).astype(BF)
    for arr in range(2):
        halves = []
        for half in range(2):
            gathered = jnp.zeros((32, 128), F32)
            for at in range(32):
                cell = half * 32 + at
                value = row(arr, cell // 8, cell % 8).astype(F32)
                moved = lane_roll(value, 4 * at + 2)
                here = (lane >= 4 * at) & (lane < 4 * at + 4)
                gathered = jnp.where(here, moved, gathered)
            halves.append(gathered.astype(BF))
        tiles = mm(jnp.concatenate(halves, axis=1), perm).astype(BF)
        out[arr, 0] = tiles[:, :128]
        out[arr, 1] = tiles[:, 128:]


def stacked_row(value, edge, cell, lane):
    before = jnp.where(lane == 0, lane_roll(edge, -cell), lane_roll(value, 1))
    after = jnp.where(lane == 127, lane_roll(edge, 63 - cell), lane_roll(value, -1))
    return jnp.concatenate([before, value, after], axis=0).astype(BF)


def edge_sum(weight, tile):
    product = mm(weight, tile)
    total = None
    for ab in range(9):
        part = lane_roll(product[ab * 32 : ab * 32 + 32], -(ab // 3 * 8 + ab % 3))
        total = part if total is None else total + part
    return total


def slope_of(value):
    sigma = jax.nn.sigmoid(value)
    return sigma, sigma * (1.0 + value * (1.0 - sigma))


def forward_taps(weight, store):
    same = ones_where(iota((32, 32), 0) == iota((32, 32), 1)).astype(BF)
    for ab in range(9):
        stack = jnp.concatenate([weight[3 * ab + c] for c in range(3)], axis=0)
        store[ab * 32 : ab * 32 + 32, :] = mm_nt(same, stack).astype(BF)


def backward_taps(weight, store):
    for ab in range(9):
        stack = [weight[26 - 3 * ab - c].astype(F32) for c in range(3)]
        store[ab * 32 : ab * 32 + 32, :] = jnp.concatenate(stack, axis=1).astype(BF)


def fine_first(
    sizes, place, own, xlo, xhi, ylo, yhi, face, face_l, face_r, w_fine_in, w_fine_out,
    keep, msg, acc, vbuf, w_z, w_d,
):
    count_x, count_y, count_z = sizes
    gx, gy, gz = place[0], place[1], place[2]
    row = rows_of(own, xlo, xhi, ylo, yhi)
    lane = iota((32, 128), 1)
    lower = lane < 64
    x_in = [gx > 0, None, None, None, None, gx < count_x - 1]
    y_in = [gy > 0, None, None, None, None, gy < count_y - 1]
    forward_taps(w_fine_in, w_z)
    backward_taps(w_fine_out, w_d)

    def factor(flag):
        return 1.0 if flag is None else jnp.where(flag, 1.0, 0.0)

    pooled = {}
    pool = ones_where(iota((32, 128), 1) // 4 == iota((32, 128), 0))
    for arr, weight in ((0, w_z), (1, w_d)):
        tile_a, tile_b = face[arr, 0].astype(F32), face[arr, 1].astype(F32)
        left_a, left_b = face_l[arr, 0].astype(F32), face_l[arr, 1].astype(F32)
        right_a, right_b = face_r[arr, 0].astype(F32), face_r[arr, 1].astype(F32)
        swapped = lane_roll(tile_b, 64)
        edge_0 = jnp.where(lower, left_a, swapped)
        edge_1 = jnp.where(lower, left_b, right_b)
        edge_2 = jnp.where(lower, swapped, right_a)
        edges = edge_sum(weight[...], jnp.concatenate([edge_0, edge_1, edge_2], axis=0).astype(BF))
        def stack_plane(xi):
            for yi in range(8):
                value = row(arr, xi, yi).astype(F32)
                line = stacked_row(value, edge_1, xi * 8 + yi, lane)
                vbuf[xi % 2, :, yi * 128 : yi * 128 + 128] = line

        stack_plane(0)
        for xi in range(8):
            if xi < 7:
                stack_plane(xi + 1)
            product = mm(weight[...], vbuf[xi % 2])
            for a in range(3):
                m = xi - a
                if 0 <= m < 6:
                    part = None
                    for b in range(3):
                        at = (3 * a + b) * 32
                        piece = product[at : at + 32, b * 128 : b * 128 + 768]
                        part = piece if part is None else part + piece
                    acc[m] = part if a == 0 else acc[m] + part
        total = jnp.zeros((32, 128), F32)
        if arr == 0:
            x_at = lane % 64 // 8
            y_at = lane % 8
            inside = jnp.where(lower, factor(gz > 0), factor(gz < count_z - 1))
            inside = inside * jnp.where(x_at == 0, factor(x_in[0]), 1.0)
            inside = inside * jnp.where(x_at == 5, factor(x_in[5]), 1.0)
            inside = inside * jnp.where(y_at == 0, factor(y_in[0]), 1.0)
            inside = inside * jnp.where(y_at == 5, factor(y_in[5]), 1.0)
            sigma, steep = slope_of(edges)
            keep[18, :, 0:128] = (edges * sigma * inside).astype(BF).astype(F32)
            keep[18, :, 128:256] = steep * inside
            for m in range(6):
                for k in range(6):
                    at = slice(k * 128, k * 128 + 128)
                    mask = factor(x_in[m]) * factor(y_in[k])
                    value = acc[m, :, at]
                    sigma, steep = slope_of(value)
                    first = (value * sigma * mask).astype(BF)
                    keep[m, :, at] = first.astype(F32)
                    keep[6 + m, :, at] = steep * mask
                    if 1 <= m < 5 and 1 <= k < 5:
                        total = total + first.astype(F32)
            total = total * (1.0 / 64.0)
        else:
            keep[18, :, 256:384] = edges
            for m in range(6):
                keep[12 + m] = acc[m]
                if 1 <= m < 5:
                    for k in range(1, 5):
                        total = total + acc[m, :, k * 128 : k * 128 + 128]
        pooled[arr] = lax.dot_general(
            pool, total, NT, preferred_element_type=F32, precision=lax.Precision.HIGHEST
        )
    msg[...] = jnp.concatenate([pooled[0], pooled[1]], axis=1).astype(BF)


def split_two(value):
    high = value.astype(BF)
    low = (value - high.astype(F32)).astype(BF)
    return jnp.concatenate([high, low], axis=0)


def lane_tiles(sizes):
    count_x, count_y, count_z = sizes
    span, lift = 128 // count_y, 32 // count_y
    first = -(-(27 * span + lift) // 128)
    second = -(-(span // count_z * 32) // 128)
    return first, second


def message_rows(sizes):
    i_mid, i_fine = 128 // sizes[0], 32 // sizes[0]
    tiles, _ = lane_tiles(sizes)
    used = tiles * i_mid + tiles * i_fine + 18 * i_fine
    return -(-used // 16) * 16


def final_rows(sizes):
    i_mid, i_fine = 128 // sizes[0], 32 // sizes[0]
    _, tiles = lane_tiles(sizes)
    used = tiles * i_mid + tiles * i_fine + 3 * (32 // (sizes[1] * sizes[2]))
    return -(-used // 16) * 16


def second(
    sizes, scale, place, recv, recv_far, own, keep,
    w_in_hbm, w_mid_hbm, w_lift_hbm, w_fine_in_hbm, w_fine_out_hbm,
    out, g_in, msg,
    raw, p3, c3, d3, e3, s2, c2, wp_in, wp_mid, bp_mid, b_in, lds, edge_rows,
    v_join, v_dz, acc, w_o, w_g, mbuf, w_in, w_mid, w_lift, w_fine_in, w_fine_out, arrived,
):
    count_x, count_y, count_z = sizes
    loads = [
        pltpu.make_async_copy(source, target, arrived.at[at])
        for at, (source, target) in enumerate(
            (
                (w_in_hbm, w_in),
                (w_mid_hbm, w_mid),
                (w_lift_hbm, w_lift),
                (w_fine_in_hbm, w_fine_in),
                (w_fine_out_hbm, w_fine_out),
            )
        )
    ]
    for load in loads:
        load.start()
    gx, gy, gz = place[0], place[1], place[2]
    rows = count_y * PITCH
    body_rows = slice(PITCH, PITCH + rows)
    deep_rows = slice(2 * PITCH, 2 * PITCH + rows)

    z_at = iota((PITCH, 128), 0)
    z_all = z_at + (gz * OWN - PAD)
    z_mask = ones_where((z_all >= 0) & (z_all < count_z * OWN))
    z_mask = jnp.concatenate([z_mask] * count_y, axis=0)
    own_mask = ones_where((z_at >= PAD) & (z_at < PAD + OWN))
    own_mask = jnp.concatenate([own_mask] * count_y, axis=0)

    for store, pads in ((p3, 1), (c3, 1), (d3, 1), (e3, 2), (c2, 1)):
        for plane in range(store.shape[0]):
            blank = jnp.zeros((pads * PITCH, store.shape[2]), BF)
            store[plane, 0 : pads * PITCH] = blank
            store[plane, pads * PITCH + rows : 2 * pads * PITCH + rows] = blank
    def inside(plane):
        at = gx + plane - PAD
        return (at >= 0) & (at < count_x), jnp.clip(at, 0, count_x - 1)

    def stacked(value):
        return jnp.concatenate([row_roll(value, 1), value, row_roll(value, -1)], axis=1).astype(BF)

    def unpack(plane):
        ok, at = inside(plane)
        valid = ones_where(ok)
        parts = []
        for y in range(count_y):
            near_by = lax.rem(gy, 2) == y % 2
            block = jnp.where(near_by, recv[at, y // 2], recv_far[at, y // 2]).astype(F32) * valid
            parts.append(block[:, :64])
            parts.append(block[:, 64:])
        whole = jnp.concatenate(parts, axis=0)
        raw[plane] = whole.astype(BF)
        first = whole[:, :32]
        around = [row_roll(first, 1), first, row_roll(first, -1), jnp.zeros((rows, 32), F32)]
        p3[plane, body_rows, :] = jnp.concatenate(around, axis=1).astype(BF)

    for load in loads:
        load.wait()
    wp_in[...] = jnp.zeros(wp_in.shape, BF)
    for a in range(3):
        for b in range(3):
            for c in range(3):
                tap = 9 * a + 3 * b + c
                side = slice(b * 128, b * 128 + 128)
                deep = slice(a * 384 + c * 128, a * 384 + c * 128 + 128)
                wp_in[a * 128 + c * 32 : a * 128 + c * 32 + 32, side] = w_in[tap]
                wp_mid[deep, side] = w_mid[tap]
                bp_mid[side, deep] = w_mid[26 - tap]
                b_in[3 * a + b, :, c * 128 : c * 128 + 128] = w_in[26 - tap]

    def taps(store, first, pair, alone, product):
        top = [store[first + a, 0 : rows + PITCH, :] for a in range(3)]
        end = [store[first + a, 2 * PITCH : 2 * PITCH + rows, :] for a in range(3)]
        both = product(jnp.concatenate(top, axis=1), pair)
        last = product(jnp.concatenate(end, axis=1), alone)
        return both[:rows, :128] + both[PITCH:, 128:] + last

    def level_2(plane):
        ok, _ = inside(plane)
        mask = z_mask * ones_where(ok)
        z_2 = taps(p3, plane - 1, wp_in[:, :256], wp_in[:, 256:], mm)
        sigma, steep = slope_of(z_2)
        s2[plane - 1] = steep * mask
        c3[plane - 1, body_rows, :] = stacked(z_2 * sigma * mask)

    lift_64 = jnp.concatenate([jnp.zeros((32, 128), BF), w_lift[...]], axis=0)

    def level_3(plane):
        ok, _ = inside(plane)
        mask = z_mask * ones_where(ok)
        z_3 = taps(c3, plane - 2, wp_mid[:, :256], wp_mid[:, 256:], mm)
        sigma, steep = slope_of(z_3)
        c2[plane - 2, body_rows, :] = (z_3 * sigma * mask).astype(BF)
        d_third = mm(raw[plane], lift_64)
        d3[plane - 2, body_rows, :] = stacked(d_third * steep)

    def level_2_back(plane):
        total = taps(d3, plane - 3, bp_mid[:256, :], bp_mid[256:, :], mm_nt)
        e3[plane - 3, deep_rows, :] = stacked(total * s2[plane - 1])

    for step in range(14):
        if step < 11:
            unpack(step)
        if 1 <= step - 1 < 10:
            level_2(step - 1)
        if 2 <= step - 2 < 9:
            level_3(step - 2)
        if 3 <= step - 3 < 8:
            level_2_back(step - 3)

    near = 3 * PITCH
    for x in range(3):
        d_pool = None
        for ab in range(9):
            start = pl.multiple_of((gy + ab % 3) * PITCH, PITCH)
            part = mm_nt(e3[x + ab // 3, pl.ds(start, near), :], b_in[ab])
            d_pool = part if d_pool is None else d_pool + part
        lifted = mm_nt(c2[2 + x, pl.ds(pl.multiple_of(gy * PITCH, PITCH), near), :], w_lift[...])
        lds[x] = jnp.concatenate([lifted, d_pool], axis=1)

    span, lift_span = 128 // count_y, 32 // count_y
    tiles, _ = lane_tiles(sizes)
    lanes = tiles * 128
    col = iota((384, 3 * span), 1)
    share = iota((384, 3 * span), 0) == col // span * 128 + col % span + gy * span
    share = ones_where(share).astype(BF)

    def shifted(store, first, pads):
        parts = []
        for a in range(3):
            picked = mm(store[first + a], share)
            for b in range(3):
                start = (pads - 1 + b) * PITCH
                parts.append(picked[start : start + rows])
        parts.append(jnp.zeros((rows, lanes - 27 * span), F32))
        return jnp.concatenate(parts, axis=1).astype(BF)

    c1_own = (c3[4, body_rows, 128:256].astype(F32) * own_mask).astype(BF)
    c2_own = (c2[3, body_rows, :].astype(F32) * own_mask).astype(BF)
    raw_own = (raw[5].astype(F32) * own_mask[:, :64]).astype(BF)
    col = iota((64, lanes), 1) - 27 * span
    pick = (iota((64, lanes), 0) == col + 32 + gy * lift_span) & (col >= 0) & (col < lift_span)
    d_lift = mm(raw[5], ones_where(pick).astype(BF)).astype(BF)
    g_mid = (mm_tn(c1_own, shifted(d3, 2, 1)) + mm_tn(c2_own, d_lift)) * scale
    g_coarse = mm_tn(raw_own, shifted(e3, 1, 2)) * scale
    i_mid, i_fine = 128 // count_x, 32 // count_x
    for x in range(count_x):
        for tile in range(tiles):
            at = slice(tile * 128, tile * 128 + 128)
            to = tile * i_mid
            mbuf[x, to : to + i_mid, :] = g_mid[x * i_mid : (x + 1) * i_mid, at]
            to = tiles * i_mid + tile * i_fine
            mbuf[x, to : to + i_fine, :] = g_coarse[x * i_fine : (x + 1) * i_fine, at]

    forward_taps(w_fine_out, w_o)
    backward_taps(w_fine_in, w_g)
    lane = iota((32, 128), 1)
    up = ones_where(iota((PITCH, 128), 0) == iota((PITCH, 128), 1) // 4 + PAD).astype(BF)
    up = jnp.concatenate([up, up], axis=0)
    spread = {}
    for x in range(3):
        for y in range(3):
            spread[x, y] = mm_tn(split_two(lds[x, y * PITCH : y * PITCH + PITCH]), up)
    edge_rows[...] = jnp.zeros(edge_rows.shape, F32)
    for side in range(2):
        for x in range(3):
            for y in range(3):
                at = side * 9 + x * 3 + y
                z = y * PITCH + (PAD - 1 if side == 0 else PAD + OWN)
                edge_rows[at : at + 1, :] = lds[x, z : z + 1, :]
    cell = iota((24, 128), 1)
    x_at, y_at = cell % 64 // 8, cell % 8
    x_of = jnp.where(x_at == 0, 0, jnp.where(x_at == 5, 2, 1))
    y_of = jnp.where(y_at == 0, 0, jnp.where(y_at == 5, 2, 1))
    edge_up = iota((24, 128), 0) == cell // 64 * 9 + x_of * 3 + y_of
    edge_up = ones_where(edge_up & (x_at < 6) & (y_at < 6))
    edge_up = jnp.concatenate([edge_up, edge_up], axis=0).astype(BF)
    spread_e = mm_tn(split_two(edge_rows[...]), edge_up)
    join_e = (keep[18, :, 0:128] + spread_e[:32]).astype(BF).astype(F32)
    dz_e = (keep[18, :, 256:384] + spread_e[32:] * (1.0 / 64.0)) * keep[18, :, 128:256]
    dz_e = dz_e.astype(BF).astype(F32)
    def stack_plane(m):
        for k in range(6):
            at = slice(k * 128, k * 128 + 128)
            over = spread[COARSE_OF[m], COARSE_OF[k]]
            join = (keep[m, :, at] + over[:32]).astype(BF).astype(F32)
            v_join[m, :, at] = stacked_row(join, join_e, m * 8 + k, lane)
            dz = (keep[12 + m, :, at] + over[32:] * (1.0 / 64.0)) * keep[6 + m, :, at]
            v_dz[m, :, at] = stacked_row(dz.astype(BF).astype(F32), dz_e, m * 8 + k, lane)

    stack_plane(0)
    for m in range(6):
        if m < 5:
            stack_plane(m + 1)
        for kind, (store, weight) in enumerate(((v_join, w_o), (v_dz, w_g))):
            product = mm(weight[...], store[m])
            for a in range(3):
                x = m - a
                if 0 <= x < 4:
                    part = None
                    for b in range(3):
                        at = (3 * a + b) * 32
                        piece = product[at : at + 32, b * 128 : b * 128 + 512]
                        part = piece if part is None else part + piece
                    if a == 0:
                        acc[kind, x] = part
                    elif a == 1:
                        acc[kind, x] = acc[kind, x] + part
                    else:
                        part = (acc[kind, x] + part).astype(BF)
                        for y in range(4):
                            (out, g_in)[kind][x, y] = part[:, y * 128 : y * 128 + 128]
    flat = [
        [jnp.concatenate([own[arr, x, y] for y in range(4)], axis=1) for x in range(4)]
        for arr in range(2)
    ]
    base = tiles * (i_mid + i_fine)
    for ab in range(9):
        a, b = ab // 3, ab % 3
        at = slice(b * 128, b * 128 + 512)
        total_o = None
        total_i = None
        for x in range(4):
            part_o = mm_nt(v_join[x + a, :, at], flat[1][x])
            part_i = mm_nt(flat[0][x], v_dz[x + a, :, at])
            total_o = part_o if total_o is None else total_o + part_o
            total_i = part_i if total_i is None else total_i + part_i
        by_tap = [total_o[c * 32 : c * 32 + 32] for c in range(3)]
        blank = jnp.zeros((32, 32), F32)
        total_o = jnp.concatenate([*by_tap, blank], axis=1)
        both = (total_o * scale, jnp.concatenate([total_i, blank], axis=1) * scale)
        for kind in range(2):
            to = base + (kind * 9 + ab) * i_fine
            for x in range(count_x):
                mbuf[x, to : to + i_fine, :] = both[kind][x * i_fine : (x + 1) * i_fine]
    used = base + 18 * i_fine
    for x in range(count_x):
        if used < mbuf.shape[1]:
            mbuf[x, used:, :] = jnp.zeros((mbuf.shape[1] - used, 128), F32)
        msg[x] = mbuf[x].astype(BF)


def gz_perm(sizes):
    count_x, count_y, count_z = sizes
    tiles, parts = lane_tiles(sizes)
    span, lift = 128 // count_y, 32 // count_y
    each, lift_each = span // count_z, lift // count_z
    perm = np.zeros((tiles * 128, count_z * parts * 128), np.float32)
    for z in range(count_z):
        base = z * parts * 128
        for tap in range(27):
            for o in range(each):
                perm[tap * span + z * each + o, base + o * 32 + 26 - tap] = 1
        for o in range(lift_each):
            perm[27 * span + z * lift_each + o, base + o * 32 + 27] = 1
    return jnp.asarray(perm, BF)


def regroup(sizes, place, recv, perm, out, buf, line):
    count_x, count_y, count_z = sizes
    gy = place[1]
    i_mid, i_fine = 128 // count_x, 32 // count_x
    tiles, parts = lane_tiles(sizes)
    total = recv[0].astype(F32)
    for x in range(1, count_x):
        total = total + recv[x].astype(F32)
    base = tiles * i_mid
    mid = jnp.concatenate([total[t * i_mid : (t + 1) * i_mid] for t in range(tiles)], axis=1)
    low = [total[base + t * i_fine : base + (t + 1) * i_fine] for t in range(tiles)]
    low = jnp.concatenate(low, axis=1)
    count = i_mid + i_fine
    padded = -(-count // 16) * 16
    blank = jnp.zeros((padded - count, tiles * 128), F32)
    coarse = jnp.concatenate([mid, low, blank], axis=0)
    moved = mm(coarse.astype(BF), perm[...])
    base = tiles * (i_mid + i_fine)
    fine = total[base : base + 18 * i_fine]
    fine = jnp.concatenate([fine, jnp.zeros((128 - 18 * i_fine, 128), F32)], axis=0)
    buf[...] = jnp.transpose(fine)
    each = 32 // (count_y * count_z)
    fine_at = parts * count
    line[...] = jnp.zeros(line.shape, F32)
    for y in range(count_y):
        own_y = ones_where(gy == y)
        for z in range(count_z):
            at = y * count_z + z
            for t in range(parts):
                piece = moved[:count, (z * parts + t) * 128 : (z * parts + t + 1) * 128] * own_y
                line[t * count : (t + 1) * count, :] = piece
            for c in range(3):
                to = fine_at + c * each
                source = c * 32 + at * each
                line[to : to + each, :] = buf[source : source + each, :]
            out[at] = line[...].astype(BF)


def finish(sizes, recv, fine_in, coarse_in, coarse_mid, lift, fine_out):
    count_x, count_y, count_z = sizes
    i_mid, i_fine = 128 // count_x, 32 // count_x
    _, parts = lane_tiles(sizes)
    total = recv[0].astype(F32)
    for at in range(1, count_y * count_z):
        total = total + recv[at].astype(F32)
    count = i_mid + i_fine
    wide = jnp.concatenate([total[t * count : (t + 1) * count] for t in range(parts)], axis=1)
    for o in range(128 // (count_y * count_z)):
        piece = wide[:, o * 32 : o * 32 + 27]
        for i in range(i_mid):
            coarse_mid[i, o : o + 1, :] = piece[i : i + 1]
        for i in range(i_fine):
            coarse_in[i, o : o + 1, :] = piece[i_mid + i : i_mid + i + 1]
    lift_each = 32 // (count_y * count_z)
    shape = (8, parts * 128)
    pick = ones_where(iota(shape, 1) == iota(shape, 0) * 32 + 27)
    exact = lax.Precision.HIGHEST
    moved = lax.dot_general(
        pick, wide[:i_mid], NT, preferred_element_type=F32, precision=exact
    )
    lift[...] = moved[:lift_each]
    base = parts * count
    cell = iota((8, 128), 1)
    keep = ones_where(iota((8, 128), 0) == cell // (9 * i_fine) * i_fine + cell % i_fine)
    cell = iota((384, 128), 0) % 128
    tap = cell // i_fine % 9 * 3 + iota((384, 128), 0) // 128
    tap = jnp.where(cell // (9 * i_fine) == 0, tap, 26 - tap)
    perm = ones_where((iota((384, 128), 1) == tap) & (cell < 18 * i_fine))
    for o in range(lift_each):
        rows = []
        for c in range(3):
            at = base + c * lift_each + o
            rows.append(jnp.broadcast_to(total[at : at + 1], (8, 128)) * keep)
        moved = jnp.dot(
            jnp.concatenate(rows, axis=1), perm, preferred_element_type=F32, precision=exact
        )
        for i in range(i_fine):
            fine_out[i, o : o + 1, :] = moved[i : i + 1, :27]
            fine_in[i, o : o + 1, :] = moved[i_fine + i : i_fine + i + 1, :27]


def from_below(value, axis):
    count = lax.axis_size(axis)
    return lax.ppermute(value, axis, [(i, i + 1) for i in range(count - 1)])


def from_above(value, axis):
    count = lax.axis_size(axis)
    return lax.ppermute(value, axis, [(i + 1, i) for i in range(count - 1)])


def shape_of(shape, dtype):
    return jax.ShapeDtypeStruct(shape, dtype)


def shards(features, cotangent, w_fine_in, w_coarse_in, w_coarse_mid, w_lift, w_fine_out):
    sizes = (lax.axis_size(GX), lax.axis_size(GY), lax.axis_size("gz"))
    count_x, count_y, count_z = sizes
    cells = count_x * count_y * count_z * 4 * 4 * 128
    scale = 1.0 / math.sqrt(cells)
    place = jnp.stack([lax.axis_index(GX), lax.axis_index(GY), lax.axis_index("gz")])
    place = place.astype(jnp.int32)

    own = jnp.stack([features, cotangent]).transpose(0, 2, 3, 1, 4)
    xlo = from_below(own[:, 2:4], GX)
    xhi = from_above(own[:, 0:2], GX)
    y_tail = jnp.concatenate([xlo[:, :, 2:4], own[:, :, 2:4], xhi[:, :, 2:4]], axis=1)
    y_head = jnp.concatenate([xlo[:, :, 0:2], own[:, :, 0:2], xhi[:, :, 0:2]], axis=1)
    ylo = from_below(y_tail, GY)
    yhi = from_above(y_head, GY)
    face = call(z_faces, shape_of((2, 2, 32, 128), BF), [], 5, False, 4)(own, xlo, xhi, ylo, yhi)
    face_l = from_below(face, "gz")
    face_r = from_above(face, "gz")
    taps = pltpu.VMEM((288, 96), BF)
    keep, msg = call(
        functools.partial(fine_first, sizes),
        (
            shape_of((19, 32, 768), F32),
            shape_of((32, 64), BF),
        ),
        [pltpu.VMEM((6, 32, 768), F32), pltpu.VMEM((2, 96, 1024), BF), taps, taps],
        11,
        True,
        10,
    )(place, own, xlo, xhi, ylo, yhi, face, face_l, face_r, w_fine_in, w_fine_out)

    z_lo = from_below(msg[24:32], "gz")
    z_hi = from_above(msg[0:8], "gz")
    window = jnp.concatenate(
        [z_lo[8 - PAD :], msg, z_hi[:PAD], jnp.zeros((PITCH - OWN - 2 * PAD, 64), BF)], axis=0
    )
    packed = jnp.concatenate([window[:24], window[24:]], axis=1)
    half_y = count_y // 2
    recv = lax.all_to_all(
        jnp.broadcast_to(packed[None], (count_x * half_y, 24, 128)),
        GX + ("gy_0",),
        split_axis=0,
        concat_axis=0,
        tiled=True,
    ).reshape(count_x, half_y, 24, 128)
    recv_far = lax.ppermute(recv, "gy_1", [(0, 1), (1, 0)])

    rows = count_y * PITCH
    wide = rows + 2 * PITCH
    out, grad_input, msg = call(
        functools.partial(second, sizes, scale),
        (
            shape_of((4, 4, 32, 128), BF),
            shape_of((4, 4, 32, 128), BF),
            shape_of((count_x, message_rows(sizes), 128), BF),
        ),
        [
            pltpu.VMEM((11, rows, 64), BF),
            pltpu.VMEM((11, wide, 128), BF),
            pltpu.VMEM((9, wide, 384), BF),
            pltpu.VMEM((7, wide, 384), BF),
            pltpu.VMEM((5, wide + 2 * PITCH, 384), BF),
            pltpu.VMEM((9, rows, 128), F32),
            pltpu.VMEM((7, wide, 128), BF),
            pltpu.VMEM((384, 384), BF),
            pltpu.VMEM((1152, 384), BF),
            pltpu.VMEM((384, 1152), BF),
            pltpu.VMEM((9, 32, 384), BF),
            pltpu.VMEM((3, 3 * PITCH, 64), F32),
            pltpu.VMEM((24, 64), F32),
            pltpu.VMEM((6, 96, 768), BF),
            pltpu.VMEM((6, 96, 768), BF),
            pltpu.VMEM((2, 4, 32, 512), F32),
            taps,
            taps,
            pltpu.VMEM((count_x, message_rows(sizes), 128), F32),
            pltpu.VMEM((27, 32, 128), BF),
            pltpu.VMEM((27, 128, 128), BF),
            pltpu.VMEM((32, 128), BF),
            pltpu.VMEM((27, 32, 32), BF),
            pltpu.VMEM((27, 32, 32), BF),
            pltpu.SemaphoreType.DMA((5,)),
        ],
        5,
        True,
        30,
        in_hbm=5,
    )(
        place, recv, recv_far, own, keep,
        w_coarse_in, w_coarse_mid, w_lift.T, w_fine_in, w_fine_out,
    )
    msg = lax.all_to_all(msg, GX, split_axis=0, concat_axis=0, tiled=True)
    msg = call(
        functools.partial(regroup, sizes),
        shape_of((count_y * count_z, final_rows(sizes), 128), BF),
        [pltpu.VMEM((128, 128), F32), pltpu.VMEM((final_rows(sizes), 128), F32)],
        3,
        True,
        6,
    )(place, msg, gz_perm(sizes))
    msg = lax.all_to_all(msg, GY + ("gz",), split_axis=0, concat_axis=0, tiled=True)
    out, grad_input, msg = lax.optimization_barrier((out, grad_input, msg))
    out = out.transpose(2, 0, 1, 3)
    grad_input = grad_input.transpose(2, 0, 1, 3)
    i_mid, i_fine = 128 // count_x, 32 // count_x
    o_mid, o_fine = 128 // (count_y * count_z), 32 // (count_y * count_z)
    grads = call(
        functools.partial(finish, sizes),
        (
            shape_of((i_fine, o_fine, 27), F32),
            shape_of((i_fine, o_mid, 27), F32),
            shape_of((i_mid, o_mid, 27), F32),
            shape_of((o_fine, i_mid), F32),
            shape_of((i_fine, o_fine, 27), F32),
        ),
        [],
        1,
        False,
        6,
        False,
    )(msg)
    fine_in, coarse_in, coarse_mid, lift, fine_out = grads
    return (
        out,
        grad_input,
        fine_in.transpose(2, 0, 1),
        coarse_in.transpose(2, 0, 1),
        coarse_mid.transpose(2, 0, 1),
        lift.T,
        fine_out.transpose(2, 0, 1),
    )


def solution(mesh):
    shape = mesh.shape
    split = Mesh(
        mesh.devices.reshape(shape["gx"] // 2, 2, shape["gy"] // 2, 2, shape["gz"]),
        GX + GY + ("gz",),
    )
    field = P(None, GX, GY, "gz")
    grad = P(None, GX, GY + ("gz",))
    return jax.shard_map(
        shards,
        mesh=split,
        in_specs=(field, field, P(), P(), P(), P(), P()),
        out_specs=(field, field, grad, grad, grad, P(GX, GY + ("gz",)), grad),
        check_vma=False,
    )
```

```python
import functools
import math

import jax
import jax.numpy as jnp
import numpy as np
from jax import lax
from jax.experimental import pallas as pl
from jax.experimental.pallas import tpu as pltpu
from jax.sharding import Mesh
from jax.sharding import PartitionSpec as P

GX = ("gx_0", "gx_1")
GY = ("gy_0", "gy_1")
INTERPRET = False
BF = jnp.bfloat16
F32 = jnp.float32
PAD = 5
OWN = 32
PITCH = 48
NT = (((1,), (1,)), ((), ()))
TN = (((0,), (0,)), ((), ()))
COARSE_OF = (0, 1, 1, 1, 1, 2)


def mm(lhs, rhs):
    return jnp.dot(lhs, rhs, preferred_element_type=F32)


def mm_nt(lhs, rhs):
    return lax.dot_general(lhs, rhs, NT, preferred_element_type=F32)


def mm_tn(lhs, rhs):
    return lax.dot_general(lhs, rhs, TN, preferred_element_type=F32)


def lane_roll(value, shift):
    return pltpu.roll(value, shift % value.shape[1], 1)


def row_roll(value, shift):
    return pltpu.roll(value, shift % value.shape[0], 0)


def call(body, out_shape, scratch, n_in, smem_first, megabytes, keep_out=True, in_hbm=0):
    spec = [pl.BlockSpec(memory_space=pltpu.VMEM)] * n_in
    if smem_first:
        spec[0] = pl.BlockSpec(memory_space=pltpu.SMEM)
    spec = spec + [pl.BlockSpec(memory_space=pl.ANY)] * in_hbm
    out_spec = pl.BlockSpec(memory_space=pltpu.VMEM) if keep_out else pl.BlockSpec()
    return pl.pallas_call(
        body,
        out_shape=out_shape,
        in_specs=spec,
        out_specs=jax.tree.map(lambda _: out_spec, out_shape),
        scratch_shapes=scratch,
        compiler_params=pltpu.CompilerParams(vmem_limit_bytes=megabytes * 1024 * 1024),
        interpret=INTERPRET,
    )


def rows_of(own, xlo, xhi, ylo, yhi):
    def row(arr, xi, yi):
        if yi < 2:
            return ylo[arr, xi, yi]
        if yi >= 6:
            return yhi[arr, xi, yi - 6]
        if xi < 2:
            return xlo[arr, xi, yi - 2]
        if xi >= 6:
            return xhi[arr, xi - 6, yi - 2]
        return own[arr, xi - 2, yi - 2]

    return row


def iota(shape, dim):
    return lax.broadcasted_iota(jnp.int32, shape, dim)


def ones_where(flag):
    return jnp.where(flag, 1.0, 0.0)


def z_faces(own, xlo, xhi, ylo, yhi, out):
    row = rows_of(own, xlo, xhi, ylo, yhi)
    lane = iota((32, 128), 1)
    column = iota((256, 256), 1)
    source = jnp.where(column < 128, 0, 1)
    source = jnp.where(column % 128 < 64, source, 3 - source)
    perm = ones_where(iota((256, 256), 0) == column % 64 * 4 + source).astype(BF)
    for arr in range(2):
        halves = []
        for half in range(2):
            gathered = jnp.zeros((32, 128), F32)
            for at in range(32):
                cell = half * 32 + at
                value = row(arr, cell // 8, cell % 8).astype(F32)
                moved = lane_roll(value, 4 * at + 2)
                here = (lane >= 4 * at) & (lane < 4 * at + 4)
                gathered = jnp.where(here, moved, gathered)
            halves.append(gathered.astype(BF))
        tiles = mm(jnp.concatenate(halves, axis=1), perm).astype(BF)
        out[arr, 0] = tiles[:, :128]
        out[arr, 1] = tiles[:, 128:]


def stacked_row(value, edge, cell, lane):
    before = jnp.where(lane == 0, lane_roll(edge, -cell), lane_roll(value, 1))
    after = jnp.where(lane == 127, lane_roll(edge, 63 - cell), lane_roll(value, -1))
    return jnp.concatenate([before, value, after], axis=0).astype(BF)


def edge_sum(weight, tile):
    product = mm(weight, tile)
    total = None
    for ab in range(9):
        part = lane_roll(product[ab * 32 : ab * 32 + 32], -(ab // 3 * 8 + ab % 3))
        total = part if total is None else total + part
    return total


def slope_of(value):
    sigma = jax.nn.sigmoid(value)
    return sigma, sigma * (1.0 + value * (1.0 - sigma))


def forward_taps(weight, store):
    same = ones_where(iota((32, 32), 0) == iota((32, 32), 1)).astype(BF)
    for ab in range(9):
        stack = jnp.concatenate([weight[3 * ab + c] for c in range(3)], axis=0)
        store[ab * 32 : ab * 32 + 32, :] = mm_nt(same, stack).astype(BF)


def backward_taps(weight, store):
    for ab in range(9):
        stack = [weight[26 - 3 * ab - c].astype(F32) for c in range(3)]
        store[ab * 32 : ab * 32 + 32, :] = jnp.concatenate(stack, axis=1).astype(BF)


def fine_first(
    sizes, place, own, xlo, xhi, ylo, yhi, face, face_l, face_r, w_fine_in, w_fine_out,
    keep, msg, acc, vbuf, w_z, w_d,
):
    count_x, count_y, count_z = sizes
    gx, gy, gz = place[0], place[1], place[2]
    row = rows_of(own, xlo, xhi, ylo, yhi)
    lane = iota((32, 128), 1)
    lower = lane < 64
    x_in = [gx > 0, None, None, None, None, gx < count_x - 1]
    y_in = [gy > 0, None, None, None, None, gy < count_y - 1]
    forward_taps(w_fine_in, w_z)
    backward_taps(w_fine_out, w_d)

    def factor(flag):
        return 1.0 if flag is None else jnp.where(flag, 1.0, 0.0)

    pooled = {}
    pool = ones_where(iota((32, 128), 1) // 4 == iota((32, 128), 0))
    for arr, weight in ((0, w_z), (1, w_d)):
        tile_a, tile_b = face[arr, 0].astype(F32), face[arr, 1].astype(F32)
        left_a, left_b = face_l[arr, 0].astype(F32), face_l[arr, 1].astype(F32)
        right_a, right_b = face_r[arr, 0].astype(F32), face_r[arr, 1].astype(F32)
        swapped = lane_roll(tile_b, 64)
        edge_0 = jnp.where(lower, left_a, swapped)
        edge_1 = jnp.where(lower, left_b, right_b)
        edge_2 = jnp.where(lower, swapped, right_a)
        edges = edge_sum(weight[...], jnp.concatenate([edge_0, edge_1, edge_2], axis=0).astype(BF))
        def stack_plane(xi):
            for yi in range(8):
                value = row(arr, xi, yi).astype(F32)
                line = stacked_row(value, edge_1, xi * 8 + yi, lane)
                vbuf[xi % 2, :, yi * 128 : yi * 128 + 128] = line

        stack_plane(0)
        for xi in range(8):
            if xi < 7:
                stack_plane(xi + 1)
            product = mm(weight[...], vbuf[xi % 2])
            for a in range(3):
                m = xi - a
                if 0 <= m < 6:
                    part = None
                    for b in range(3):
                        at = (3 * a + b) * 32
                        piece = product[at : at + 32, b * 128 : b * 128 + 768]
                        part = piece if part is None else part + piece
                    acc[m] = part if a == 0 else acc[m] + part
        total = jnp.zeros((32, 128), F32)
        if arr == 0:
            x_at = lane % 64 // 8
            y_at = lane % 8
            inside = jnp.where(lower, factor(gz > 0), factor(gz < count_z - 1))
            inside = inside * jnp.where(x_at == 0, factor(x_in[0]), 1.0)
            inside = inside * jnp.where(x_at == 5, factor(x_in[5]), 1.0)
            inside = inside * jnp.where(y_at == 0, factor(y_in[0]), 1.0)
            inside = inside * jnp.where(y_at == 5, factor(y_in[5]), 1.0)
            sigma, steep = slope_of(edges)
            keep[18, :, 0:128] = (edges * sigma * inside).astype(BF).astype(F32)
            keep[18, :, 128:256] = steep * inside
            for m in range(6):
                for k in range(6):
                    at = slice(k * 128, k * 128 + 128)
                    mask = factor(x_in[m]) * factor(y_in[k])
                    value = acc[m, :, at]
                    sigma, steep = slope_of(value)
                    first = (value * sigma * mask).astype(BF)
                    keep[m, :, at] = first.astype(F32)
                    keep[6 + m, :, at] = steep * mask
                    if 1 <= m < 5 and 1 <= k < 5:
                        total = total + first.astype(F32)
            total = total * (1.0 / 64.0)
        else:
            keep[18, :, 256:384] = edges
            for m in range(6):
                keep[12 + m] = acc[m]
                if 1 <= m < 5:
                    for k in range(1, 5):
                        total = total + acc[m, :, k * 128 : k * 128 + 128]
        pooled[arr] = lax.dot_general(
            pool, total, NT, preferred_element_type=F32, precision=lax.Precision.HIGHEST
        )
    msg[...] = jnp.concatenate([pooled[0], pooled[1]], axis=1).astype(BF)


def split_two(value):
    high = value.astype(BF)
    low = (value - high.astype(F32)).astype(BF)
    return jnp.concatenate([high, low], axis=0)


def lane_tiles(sizes):
    count_x, count_y, count_z = sizes
    span, lift = 128 // count_y, 32 // count_y
    first = -(-(27 * span + lift) // 128)
    second = -(-(span // count_z * 32) // 128)
    return first, second


def message_rows(sizes):
    i_mid, i_fine = 128 // sizes[0], 32 // sizes[0]
    tiles, _ = lane_tiles(sizes)
    used = tiles * i_mid + tiles * i_fine + 18 * i_fine
    return -(-used // 16) * 16


def final_rows(sizes):
    i_mid, i_fine = 128 // sizes[0], 32 // sizes[0]
    _, tiles = lane_tiles(sizes)
    used = tiles * i_mid + tiles * i_fine + 3 * (32 // (sizes[1] * sizes[2]))
    return -(-used // 16) * 16


def second(
    sizes, scale, place, recv, recv_far, own, keep,
    w_in_hbm, w_mid_hbm, w_lift_hbm, w_fine_in_hbm, w_fine_out_hbm,
    out, g_in, msg,
    raw, p3, c3, d3, e3, s2, c2, wp_in, wp_mid, bp_mid, b_in, lds, edge_rows,
    v_join, v_dz, acc, w_o, w_g, mbuf, w_in, w_mid, w_lift, w_fine_in, w_fine_out, arrived,
):
    count_x, count_y, count_z = sizes
    loads = [
        pltpu.make_async_copy(source, target, arrived.at[at])
        for at, (source, target) in enumerate(
            (
                (w_in_hbm, w_in),
                (w_mid_hbm, w_mid),
                (w_lift_hbm, w_lift),
                (w_fine_in_hbm, w_fine_in),
                (w_fine_out_hbm, w_fine_out),
            )
        )
    ]
    for load in loads:
        load.start()
    gx, gy, gz = place[0], place[1], place[2]
    rows = count_y * PITCH
    body_rows = slice(PITCH, PITCH + rows)
    deep_rows = slice(2 * PITCH, 2 * PITCH + rows)

    z_at = iota((PITCH, 128), 0)
    z_all = z_at + (gz * OWN - PAD)
    z_mask = ones_where((z_all >= 0) & (z_all < count_z * OWN))
    z_mask = jnp.concatenate([z_mask] * count_y, axis=0)
    own_mask = ones_where((z_at >= PAD) & (z_at < PAD + OWN))
    own_mask = jnp.concatenate([own_mask] * count_y, axis=0)

    for store, pads in ((p3, 1), (c3, 1), (d3, 1), (e3, 2), (c2, 1)):
        for plane in range(store.shape[0]):
            blank = jnp.zeros((pads * PITCH, store.shape[2]), BF)
            store[plane, 0 : pads * PITCH] = blank
            store[plane, pads * PITCH + rows : 2 * pads * PITCH + rows] = blank
    def inside(plane):
        at = gx + plane - PAD
        return (at >= 0) & (at < count_x), jnp.clip(at, 0, count_x - 1)

    def stacked(value):
        return jnp.concatenate([row_roll(value, 1), value, row_roll(value, -1)], axis=1).astype(BF)

    def unpack(plane):
        ok, at = inside(plane)
        valid = ones_where(ok)
        parts = []
        for y in range(count_y):
            near_by = lax.rem(gy, 2) == y % 2
            block = jnp.where(near_by, recv[at, y // 2], recv_far[at, y // 2]).astype(F32) * valid
            parts.append(block[:, :64])
            parts.append(block[:, 64:])
        whole = jnp.concatenate(parts, axis=0)
        raw[plane] = whole.astype(BF)
        first = whole[:, :32]
        around = [row_roll(first, 1), first, row_roll(first, -1), jnp.zeros((rows, 32), F32)]
        p3[plane, body_rows, :] = jnp.concatenate(around, axis=1).astype(BF)

    tap_list = [(a, b, c) for a in range(3) for b in range(3) for c in range(3)]

    def weights_in():
        loads[0].wait()
        wp_in[...] = jnp.zeros(wp_in.shape, BF)
        for tap, (a, b, c) in enumerate(tap_list):
            deep = a * 128 + c * 32
            wp_in[deep : deep + 32, b * 128 : b * 128 + 128] = w_in[tap]
            b_in[3 * a + b, :, c * 128 : c * 128 + 128] = w_in[26 - tap]

    def weights_mid():
        loads[1].wait()
        for tap, (a, b, c) in enumerate(tap_list):
            side = slice(b * 128, b * 128 + 128)
            deep = slice(a * 384 + c * 128, a * 384 + c * 128 + 128)
            wp_mid[deep, side] = w_mid[tap]
            bp_mid[side, deep] = w_mid[26 - tap]

    def taps(store, first, pair, alone, product):
        top = [store[first + a, 0 : rows + PITCH, :] for a in range(3)]
        end = [store[first + a, 2 * PITCH : 2 * PITCH + rows, :] for a in range(3)]
        both = product(jnp.concatenate(top, axis=1), pair)
        last = product(jnp.concatenate(end, axis=1), alone)
        return both[:rows, :128] + both[PITCH:, 128:] + last

    def level_2(plane):
        ok, _ = inside(plane)
        mask = z_mask * ones_where(ok)
        z_2 = taps(p3, plane - 1, wp_in[:, :256], wp_in[:, 256:], mm)
        sigma, steep = slope_of(z_2)
        s2[plane - 1] = steep * mask
        c3[plane - 1, body_rows, :] = stacked(z_2 * sigma * mask)

    def level_3(plane):
        ok, _ = inside(plane)
        mask = z_mask * ones_where(ok)
        z_3 = taps(c3, plane - 2, wp_mid[:, :256], wp_mid[:, 256:], mm)
        sigma, steep = slope_of(z_3)
        c2[plane - 2, body_rows, :] = (z_3 * sigma * mask).astype(BF)
        lift_64 = jnp.concatenate([jnp.zeros((32, 128), BF), w_lift[...]], axis=0)
        d_third = mm(raw[plane], lift_64)
        d3[plane - 2, body_rows, :] = stacked(d_third * steep)

    def level_2_back(plane):
        total = taps(d3, plane - 3, bp_mid[:256, :], bp_mid[256:, :], mm_nt)
        e3[plane - 3, deep_rows, :] = stacked(total * s2[plane - 1])

    for step in range(14):
        if step < 11:
            unpack(step)
        if step == 1:
            weights_in()
        if step == 3:
            weights_mid()
            loads[2].wait()
        if 1 <= step - 1 < 10:
            level_2(step - 1)
        if 2 <= step - 2 < 9:
            level_3(step - 2)
        if 3 <= step - 3 < 8:
            level_2_back(step - 3)

    near = 3 * PITCH
    for x in range(3):
        d_pool = None
        for ab in range(9):
            start = pl.multiple_of((gy + ab % 3) * PITCH, PITCH)
            part = mm_nt(e3[x + ab // 3, pl.ds(start, near), :], b_in[ab])
            d_pool = part if d_pool is None else d_pool + part
        lifted = mm_nt(c2[2 + x, pl.ds(pl.multiple_of(gy * PITCH, PITCH), near), :], w_lift[...])
        lds[x] = jnp.concatenate([lifted, d_pool], axis=1)

    span, lift_span = 128 // count_y, 32 // count_y
    tiles, _ = lane_tiles(sizes)
    lanes = tiles * 128
    col = iota((384, 3 * span), 1)
    share = iota((384, 3 * span), 0) == col // span * 128 + col % span + gy * span
    share = ones_where(share).astype(BF)

    def shifted(store, first, pads):
        parts = []
        for a in range(3):
            picked = mm(store[first + a], share)
            for b in range(3):
                start = (pads - 1 + b) * PITCH
                parts.append(picked[start : start + rows])
        parts.append(jnp.zeros((rows, lanes - 27 * span), F32))
        return jnp.concatenate(parts, axis=1).astype(BF)

    c1_own = (c3[4, body_rows, 128:256].astype(F32) * own_mask).astype(BF)
    c2_own = (c2[3, body_rows, :].astype(F32) * own_mask).astype(BF)
    raw_own = (raw[5].astype(F32) * own_mask[:, :64]).astype(BF)
    col = iota((64, lanes), 1) - 27 * span
    pick = (iota((64, lanes), 0) == col + 32 + gy * lift_span) & (col >= 0) & (col < lift_span)
    d_lift = mm(raw[5], ones_where(pick).astype(BF)).astype(BF)
    g_mid = (mm_tn(c1_own, shifted(d3, 2, 1)) + mm_tn(c2_own, d_lift)) * scale
    g_coarse = mm_tn(raw_own, shifted(e3, 1, 2)) * scale
    i_mid, i_fine = 128 // count_x, 32 // count_x
    for x in range(count_x):
        for tile in range(tiles):
            at = slice(tile * 128, tile * 128 + 128)
            to = tile * i_mid
            mbuf[x, to : to + i_mid, :] = g_mid[x * i_mid : (x + 1) * i_mid, at]
            to = tiles * i_mid + tile * i_fine
            mbuf[x, to : to + i_fine, :] = g_coarse[x * i_fine : (x + 1) * i_fine, at]

    loads[3].wait()
    loads[4].wait()
    forward_taps(w_fine_out, w_o)
    backward_taps(w_fine_in, w_g)
    lane = iota((32, 128), 1)
    up = ones_where(iota((PITCH, 128), 0) == iota((PITCH, 128), 1) // 4 + PAD).astype(BF)
    up = jnp.concatenate([up, up], axis=0)
    spread = {}
    for x in range(3):
        for y in range(3):
            spread[x, y] = mm_tn(split_two(lds[x, y * PITCH : y * PITCH + PITCH]), up)
    edge_rows[...] = jnp.zeros(edge_rows.shape, F32)
    for side in range(2):
        for x in range(3):
            for y in range(3):
                at = side * 9 + x * 3 + y
                z = y * PITCH + (PAD - 1 if side == 0 else PAD + OWN)
                edge_rows[at : at + 1, :] = lds[x, z : z + 1, :]
    cell = iota((24, 128), 1)
    x_at, y_at = cell % 64 // 8, cell % 8
    x_of = jnp.where(x_at == 0, 0, jnp.where(x_at == 5, 2, 1))
    y_of = jnp.where(y_at == 0, 0, jnp.where(y_at == 5, 2, 1))
    edge_up = iota((24, 128), 0) == cell // 64 * 9 + x_of * 3 + y_of
    edge_up = ones_where(edge_up & (x_at < 6) & (y_at < 6))
    edge_up = jnp.concatenate([edge_up, edge_up], axis=0).astype(BF)
    spread_e = mm_tn(split_two(edge_rows[...]), edge_up)
    join_e = (keep[18, :, 0:128] + spread_e[:32]).astype(BF).astype(F32)
    dz_e = (keep[18, :, 256:384] + spread_e[32:] * (1.0 / 64.0)) * keep[18, :, 128:256]
    dz_e = dz_e.astype(BF).astype(F32)
    def stack_plane(m):
        for k in range(6):
            at = slice(k * 128, k * 128 + 128)
            over = spread[COARSE_OF[m], COARSE_OF[k]]
            join = (keep[m, :, at] + over[:32]).astype(BF).astype(F32)
            v_join[m, :, at] = stacked_row(join, join_e, m * 8 + k, lane)
            dz = (keep[12 + m, :, at] + over[32:] * (1.0 / 64.0)) * keep[6 + m, :, at]
            v_dz[m, :, at] = stacked_row(dz.astype(BF).astype(F32), dz_e, m * 8 + k, lane)

    stack_plane(0)
    for m in range(6):
        if m < 5:
            stack_plane(m + 1)
        for kind, (store, weight) in enumerate(((v_join, w_o), (v_dz, w_g))):
            product = mm(weight[...], store[m])
            for a in range(3):
                x = m - a
                if 0 <= x < 4:
                    part = None
                    for b in range(3):
                        at = (3 * a + b) * 32
                        piece = product[at : at + 32, b * 128 : b * 128 + 512]
                        part = piece if part is None else part + piece
                    if a == 0:
                        acc[kind, x] = part
                    elif a == 1:
                        acc[kind, x] = acc[kind, x] + part
                    else:
                        part = (acc[kind, x] + part).astype(BF)
                        for y in range(4):
                            (out, g_in)[kind][x, y] = part[:, y * 128 : y * 128 + 128]
    flat = [
        [jnp.concatenate([own[arr, x, y] for y in range(4)], axis=1) for x in range(4)]
        for arr in range(2)
    ]
    base = tiles * (i_mid + i_fine)
    for ab in range(9):
        a, b = ab // 3, ab % 3
        at = slice(b * 128, b * 128 + 512)
        total_o = None
        total_i = None
        for x in range(4):
            part_o = mm_nt(v_join[x + a, :, at], flat[1][x])
            part_i = mm_nt(flat[0][x], v_dz[x + a, :, at])
            total_o = part_o if total_o is None else total_o + part_o
            total_i = part_i if total_i is None else total_i + part_i
        by_tap = [total_o[c * 32 : c * 32 + 32] for c in range(3)]
        blank = jnp.zeros((32, 32), F32)
        total_o = jnp.concatenate([*by_tap, blank], axis=1)
        both = (total_o * scale, jnp.concatenate([total_i, blank], axis=1) * scale)
        for kind in range(2):
            to = base + (kind * 9 + ab) * i_fine
            for x in range(count_x):
                mbuf[x, to : to + i_fine, :] = both[kind][x * i_fine : (x + 1) * i_fine]
    used = base + 18 * i_fine
    for x in range(count_x):
        if used < mbuf.shape[1]:
            mbuf[x, used:, :] = jnp.zeros((mbuf.shape[1] - used, 128), F32)
        msg[x] = mbuf[x].astype(BF)


def gz_perm(sizes):
    count_x, count_y, count_z = sizes
    tiles, parts = lane_tiles(sizes)
    span, lift = 128 // count_y, 32 // count_y
    each, lift_each = span // count_z, lift // count_z
    perm = np.zeros((tiles * 128, count_z * parts * 128), np.float32)
    for z in range(count_z):
        base = z * parts * 128
        for tap in range(27):
            for o in range(each):
                perm[tap * span + z * each + o, base + o * 32 + 26 - tap] = 1
        for o in range(lift_each):
            perm[27 * span + z * lift_each + o, base + o * 32 + 27] = 1
    return jnp.asarray(perm, BF)


def regroup(sizes, place, recv, perm, out, buf, line):
    count_x, count_y, count_z = sizes
    gy = place[1]
    i_mid, i_fine = 128 // count_x, 32 // count_x
    tiles, parts = lane_tiles(sizes)
    total = recv[0].astype(F32)
    for x in range(1, count_x):
        total = total + recv[x].astype(F32)
    base = tiles * i_mid
    mid = jnp.concatenate([total[t * i_mid : (t + 1) * i_mid] for t in range(tiles)], axis=1)
    low = [total[base + t * i_fine : base + (t + 1) * i_fine] for t in range(tiles)]
    low = jnp.concatenate(low, axis=1)
    count = i_mid + i_fine
    padded = -(-count // 16) * 16
    blank = jnp.zeros((padded - count, tiles * 128), F32)
    coarse = jnp.concatenate([mid, low, blank], axis=0)
    moved = mm(coarse.astype(BF), perm[...])
    base = tiles * (i_mid + i_fine)
    fine = total[base : base + 18 * i_fine]
    fine = jnp.concatenate([fine, jnp.zeros((128 - 18 * i_fine, 128), F32)], axis=0)
    buf[...] = jnp.transpose(fine)
    each = 32 // (count_y * count_z)
    fine_at = parts * count
    line[...] = jnp.zeros(line.shape, F32)
    for y in range(count_y):
        own_y = ones_where(gy == y)
        for z in range(count_z):
            at = y * count_z + z
            for t in range(parts):
                piece = moved[:count, (z * parts + t) * 128 : (z * parts + t + 1) * 128] * own_y
                line[t * count : (t + 1) * count, :] = piece
            for c in range(3):
                to = fine_at + c * each
                source = c * 32 + at * each
                line[to : to + each, :] = buf[source : source + each, :]
            out[at] = line[...].astype(BF)


def finish(sizes, recv, fine_in, coarse_in, coarse_mid, lift, fine_out):
    count_x, count_y, count_z = sizes
    i_mid, i_fine = 128 // count_x, 32 // count_x
    _, parts = lane_tiles(sizes)
    total = recv[0].astype(F32)
    for at in range(1, count_y * count_z):
        total = total + recv[at].astype(F32)
    count = i_mid + i_fine
    wide = jnp.concatenate([total[t * count : (t + 1) * count] for t in range(parts)], axis=1)
    for o in range(128 // (count_y * count_z)):
        piece = wide[:, o * 32 : o * 32 + 27]
        for i in range(i_mid):
            coarse_mid[i, o : o + 1, :] = piece[i : i + 1]
        for i in range(i_fine):
            coarse_in[i, o : o + 1, :] = piece[i_mid + i : i_mid + i + 1]
    lift_each = 32 // (count_y * count_z)
    shape = (8, parts * 128)
    pick = ones_where(iota(shape, 1) == iota(shape, 0) * 32 + 27)
    exact = lax.Precision.HIGHEST
    moved = lax.dot_general(
        pick, wide[:i_mid], NT, preferred_element_type=F32, precision=exact
    )
    lift[...] = moved[:lift_each]
    base = parts * count
    cell = iota((8, 128), 1)
    keep = ones_where(iota((8, 128), 0) == cell // (9 * i_fine) * i_fine + cell % i_fine)
    cell = iota((384, 128), 0) % 128
    tap = cell // i_fine % 9 * 3 + iota((384, 128), 0) // 128
    tap = jnp.where(cell // (9 * i_fine) == 0, tap, 26 - tap)
    perm = ones_where((iota((384, 128), 1) == tap) & (cell < 18 * i_fine))
    for o in range(lift_each):
        rows = []
        for c in range(3):
            at = base + c * lift_each + o
            rows.append(jnp.broadcast_to(total[at : at + 1], (8, 128)) * keep)
        moved = jnp.dot(
            jnp.concatenate(rows, axis=1), perm, preferred_element_type=F32, precision=exact
        )
        for i in range(i_fine):
            fine_out[i, o : o + 1, :] = moved[i : i + 1, :27]
            fine_in[i, o : o + 1, :] = moved[i_fine + i : i_fine + i + 1, :27]


def from_below(value, axis):
    count = lax.axis_size(axis)
    return lax.ppermute(value, axis, [(i, i + 1) for i in range(count - 1)])


def from_above(value, axis):
    count = lax.axis_size(axis)
    return lax.ppermute(value, axis, [(i + 1, i) for i in range(count - 1)])


def shape_of(shape, dtype):
    return jax.ShapeDtypeStruct(shape, dtype)


def shards(features, cotangent, w_fine_in, w_coarse_in, w_coarse_mid, w_lift, w_fine_out):
    sizes = (lax.axis_size(GX), lax.axis_size(GY), lax.axis_size("gz"))
    count_x, count_y, count_z = sizes
    cells = count_x * count_y * count_z * 4 * 4 * 128
    scale = 1.0 / math.sqrt(cells)
    place = jnp.stack([lax.axis_index(GX), lax.axis_index(GY), lax.axis_index("gz")])
    place = place.astype(jnp.int32)

    own = jnp.stack([features, cotangent]).transpose(0, 2, 3, 1, 4)
    xlo = from_below(own[:, 2:4], GX)
    xhi = from_above(own[:, 0:2], GX)
    y_tail = jnp.concatenate([xlo[:, :, 2:4], own[:, :, 2:4], xhi[:, :, 2:4]], axis=1)
    y_head = jnp.concatenate([xlo[:, :, 0:2], own[:, :, 0:2], xhi[:, :, 0:2]], axis=1)
    ylo = from_below(y_tail, GY)
    yhi = from_above(y_head, GY)
    face = call(z_faces, shape_of((2, 2, 32, 128), BF), [], 5, False, 4)(own, xlo, xhi, ylo, yhi)
    face_l = from_below(face, "gz")
    face_r = from_above(face, "gz")
    taps = pltpu.VMEM((288, 96), BF)
    keep, msg = call(
        functools.partial(fine_first, sizes),
        (
            shape_of((19, 32, 768), F32),
            shape_of((32, 64), BF),
        ),
        [pltpu.VMEM((6, 32, 768), F32), pltpu.VMEM((2, 96, 1024), BF), taps, taps],
        11,
        True,
        10,
    )(place, own, xlo, xhi, ylo, yhi, face, face_l, face_r, w_fine_in, w_fine_out)

    z_lo = from_below(msg[24:32], "gz")
    z_hi = from_above(msg[0:8], "gz")
    window = jnp.concatenate(
        [z_lo[8 - PAD :], msg, z_hi[:PAD], jnp.zeros((PITCH - OWN - 2 * PAD, 64), BF)], axis=0
    )
    packed = jnp.concatenate([window[:24], window[24:]], axis=1)
    half_y = count_y // 2
    recv = lax.all_to_all(
        jnp.broadcast_to(packed[None], (count_x * half_y, 24, 128)),
        GX + ("gy_0",),
        split_axis=0,
        concat_axis=0,
        tiled=True,
    ).reshape(count_x, half_y, 24, 128)
    recv_far = lax.ppermute(recv, "gy_1", [(0, 1), (1, 0)])

    rows = count_y * PITCH
    wide = rows + 2 * PITCH
    out, grad_input, msg = call(
        functools.partial(second, sizes, scale),
        (
            shape_of((4, 4, 32, 128), BF),
            shape_of((4, 4, 32, 128), BF),
            shape_of((count_x, message_rows(sizes), 128), BF),
        ),
        [
            pltpu.VMEM((11, rows, 64), BF),
            pltpu.VMEM((11, wide, 128), BF),
            pltpu.VMEM((9, wide, 384), BF),
            pltpu.VMEM((7, wide, 384), BF),
            pltpu.VMEM((5, wide + 2 * PITCH, 384), BF),
            pltpu.VMEM((9, rows, 128), F32),
            pltpu.VMEM((7, wide, 128), BF),
            pltpu.VMEM((384, 384), BF),
            pltpu.VMEM((1152, 384), BF),
            pltpu.VMEM((384, 1152), BF),
            pltpu.VMEM((9, 32, 384), BF),
            pltpu.VMEM((3, 3 * PITCH, 64), F32),
            pltpu.VMEM((24, 64), F32),
            pltpu.VMEM((6, 96, 768), BF),
            pltpu.VMEM((6, 96, 768), BF),
            pltpu.VMEM((2, 4, 32, 512), F32),
            taps,
            taps,
            pltpu.VMEM((count_x, message_rows(sizes), 128), F32),
            pltpu.VMEM((27, 32, 128), BF),
            pltpu.VMEM((27, 128, 128), BF),
            pltpu.VMEM((32, 128), BF),
            pltpu.VMEM((27, 32, 32), BF),
            pltpu.VMEM((27, 32, 32), BF),
            pltpu.SemaphoreType.DMA((5,)),
        ],
        5,
        True,
        30,
        in_hbm=5,
    )(
        place, recv, recv_far, own, keep,
        w_coarse_in, w_coarse_mid, w_lift.T, w_fine_in, w_fine_out,
    )
    out = out.transpose(2, 0, 1, 3)
    grad_input = grad_input.transpose(2, 0, 1, 3)

    msg = lax.all_to_all(msg, GX, split_axis=0, concat_axis=0, tiled=True)
    msg = call(
        functools.partial(regroup, sizes),
        shape_of((count_y * count_z, final_rows(sizes), 128), BF),
        [pltpu.VMEM((128, 128), F32), pltpu.VMEM((final_rows(sizes), 128), F32)],
        3,
        True,
        6,
    )(place, msg, gz_perm(sizes))
    msg = lax.all_to_all(msg, GY + ("gz",), split_axis=0, concat_axis=0, tiled=True)
    i_mid, i_fine = 128 // count_x, 32 // count_x
    o_mid, o_fine = 128 // (count_y * count_z), 32 // (count_y * count_z)
    grads = call(
        functools.partial(finish, sizes),
        (
            shape_of((i_fine, o_fine, 27), F32),
            shape_of((i_fine, o_mid, 27), F32),
            shape_of((i_mid, o_mid, 27), F32),
            shape_of((o_fine, i_mid), F32),
            shape_of((i_fine, o_fine, 27), F32),
        ),
        [],
        1,
        False,
        6,
        False,
    )(msg)
    fine_in, coarse_in, coarse_mid, lift, fine_out = grads
    return (
        out,
        grad_input,
        fine_in.transpose(2, 0, 1),
        coarse_in.transpose(2, 0, 1),
        coarse_mid.transpose(2, 0, 1),
        lift.T,
        fine_out.transpose(2, 0, 1),
    )


def solution(mesh):
    shape = mesh.shape
    split = Mesh(
        mesh.devices.reshape(shape["gx"] // 2, 2, shape["gy"] // 2, 2, shape["gz"]),
        GX + GY + ("gz",),
    )
    field = P(None, GX, GY, "gz")
    grad = P(None, GX, GY + ("gz",))
    return jax.shard_map(
        shards,
        mesh=split,
        in_specs=(field, field, P(), P(), P(), P(), P()),
        out_specs=(field, field, grad, grad, grad, P(GX, GY + ("gz",)), grad),
        check_vma=False,
    )
```
